32 devices in a mesh: grp: 8 (over z, y), in: 4 (over x, core).
Axes of the slice: x: 2, y: 2, z: 4, core: 2. Of those that a mesh axis runs over, the one named last changes fastest.
Arguments:
- picture_embeds: bfloat16 [4096, 1152], P(('grp', 'in')), may hold values from -0.1875 to 0.1875
- caption_embeds: bfloat16 [4096, 1152], P(('grp', 'in')), may hold values from -0.1875 to 0.1875
- sharpness_factor: float32 [1], replicated, may hold values from 10 to 30
- additive_shift_term: float32 [1], replicated, may hold values from -4 to -2
Outputs:
- image_grad: bfloat16 [4096, 1152], P(('grp', 'in'))
- text_grad: bfloat16 [4096, 1152], P(('grp', 'in'))
The draws below stay inside these ranges and needn't reach their ends.
All inputs are finite; a program needn't handle non-finite values.
Results may differ from the reference program's by a relative error of at most 0.0046.
Values may be sent and summed in bfloat16 or wider, within the bound.
No kernel may reach another device: no remote copies, remote signals or barrier semaphores. Data moves between devices by JAX's collectives and lax.ppermute only.
A program may use at most 64 MiB of HBM per device.

```python
import math
import jax
import jax.numpy as jnp
from jax import lax

D = 1152
ROWS_PER_UNIT = 128
STEPS = 2
PAIRS = 4096
N_GRP = 8
N_IN = 4


def steps_of(key, shape, split, smallest, largest):
    def one(position, shards_of):
        heights = jax.random.uniform(jax.random.fold_in(jax.random.fold_in(key, 6), position), (shards_of,), jnp.float32, smallest / len(split), largest / len(split))
        return jnp.repeat(jnp.exp(heights), shape[position] // shards_of).reshape((-1,) + (1,) * (len(shape) - position - 1))

    factor_of = one(*split[0])
    for cut in split[1:]:
        factor_of = factor_of * one(*cut)
    return factor_of


def gaussian(stream_key, extent, spread, limit, cuts=(), held_as=jnp.bfloat16):
    gain = steps_of(stream_key, extent, cuts, -0.22, 0.18) if cuts else 1.0
    values = jax.random.normal(stream_key, extent, jnp.float32) * spread * gain
    return jnp.minimum(jnp.maximum(values, -limit), limit).astype(held_as)


def setup_inputs(seed: int = 0) -> dict:
    seeds = jax.random.split(jax.random.key(seed), 5)
    return {
        "picture_embeds": gaussian(seeds[0], (PAIRS, D), D ** -0.5, 0.1875, ((0, 32),)),
        "caption_embeds": gaussian(seeds[1], (PAIRS, D), D ** -0.5, 0.1875, ((0, 32),)),
        "sharpness_factor": jnp.clip(jnp.exp(jax.random.uniform(seeds[2], (1,), jnp.float32, math.log(10.0), math.log(30.0))), 10.0, 30.0),
        "additive_shift_term": jnp.clip(jax.random.uniform(seeds[3], (1,), jnp.float32, -4.0, -2.0), -4.0, -2.0),
    }


def reference(picture_embeds, caption_embeds, sharpness_factor, additive_shift_term):
    group_rows = N_IN * ROWS_PER_UNIT
    image_groups = picture_embeds.reshape(N_GRP, group_rows, D)
    text_groups = caption_embeds.reshape(N_GRP, group_rows, D)
    sharpness_scalar = sharpness_factor[0]
    additive_term_scalar = additive_shift_term[0]
    identity = jnp.eye(group_rows, dtype=jnp.float32)
    image_total = jnp.zeros((N_GRP, group_rows, D), jnp.float32)
    text_total = jnp.zeros((N_GRP, group_rows, D), jnp.float32)
    for batch_start_index in range(STEPS):
        partners = jnp.roll(text_groups, batch_start_index, axis=0)
        matching_mask = identity * (1.0 if batch_start_index == 0 else 0.0)

        def pair_block(operands):
            picture_slice, caption_slice = operands
            similarity_matrix = sharpness_scalar * jnp.dot(picture_slice, caption_slice.T, preferred_element_type=jnp.float32) + additive_term_scalar
            label_signs = (sharpness_scalar * (jax.nn.sigmoid(similarity_matrix) - matching_mask)).astype(jnp.bfloat16)
            image_terms = jnp.dot(label_signs, caption_slice, preferred_element_type=jnp.float32)
            text_terms = jnp.dot(label_signs.T, picture_slice, preferred_element_type=jnp.float32)
            return image_terms, text_terms

        image_terms, text_terms = lax.map(pair_block, (image_groups, partners))
        image_total = image_total + image_terms
        text_total = text_total + jnp.roll(text_terms, -batch_start_index, axis=0)
    image_grad = image_total.reshape(N_GRP * group_rows, D).astype(jnp.bfloat16)
    text_grad = text_total.reshape(N_GRP * group_rows, D).astype(jnp.bfloat16)
    return image_grad, text_grad
```

```python
import jax
import jax.numpy as jnp
from jax import lax
from jax.sharding import PartitionSpec as P

CORES = 2


def moved(array, axis, target):
    peers = lax.axis_size(axis)
    return lax.ppermute(array, axis, [(i, target(i) % peers) for i in range(peers)])


def swapped(array):
    return moved(array, "in", lambda i: i ^ 1)


def pulled(rows, others, scale, shift, diagonal):
    total = None
    for position, other in enumerate(others):
        logits = scale * jnp.dot(rows, other.T, preferred_element_type=jnp.float32) + shift
        slope = jax.nn.sigmoid(logits)
        if diagonal and position == 0:
            slope = slope - jnp.eye(rows.shape[0], dtype=jnp.float32)
        weights = (scale * slope).astype(jnp.bfloat16)
        term = jnp.dot(weights, other, preferred_element_type=jnp.float32)
        total = term if total is None else total + term
    return total


def shards(images, texts, sharpness_factor, additive_shift_term):
    scale = sharpness_factor[0]
    shift = additive_shift_term[0]
    chips = lax.axis_size("in") // CORES

    near_images = [moved(images, "in", lambda i, k=k: i - CORES * k) for k in range(1, chips)]
    back_texts = moved(texts, "grp", lambda i: i + 1)
    own_images = [images, swapped(images)]
    own_texts = [texts, swapped(texts)]
    far_images = [swapped(block) for block in near_images]
    all_texts = own_texts + [back_texts, swapped(back_texts)]
    all_images = own_images + near_images + far_images

    sent_images = [
        moved(
            pulled(block, all_texts, scale, shift, False).astype(jnp.bfloat16),
            "in",
            lambda i, k=k: i + CORES * k,
        )
        for k, block in enumerate(near_images, 1)
    ]
    sent_texts = moved(
        pulled(back_texts, all_images, scale, shift, False).astype(jnp.bfloat16),
        "grp",
        lambda i: i - 1,
    )
    image_total = pulled(images, all_texts, scale, shift, True)
    text_total = pulled(texts, all_images, scale, shift, True)
    for block in sent_images:
        image_total = image_total + block.astype(jnp.float32)
    text_total = text_total + sent_texts.astype(jnp.float32)
    return image_total.astype(jnp.bfloat16), text_total.astype(jnp.bfloat16)


def solution(mesh):
    rows = P(("grp", "in"), None)
    return jax.shard_map(
        shards,
        mesh=mesh,
        in_specs=(rows, rows, P(), P()),
        out_specs=(rows, rows),
        check_vma=False,
    )
```

```python
import jax
import jax.numpy as jnp
from jax import lax
from jax.experimental import pallas as pl
from jax.experimental.pallas import tpu as pltpu
from jax.sharding import PartitionSpec as P

CORES = 2


def moved(array, axis, target):
    peers = lax.axis_size(axis)
    return lax.ppermute(array, axis, [(i, target(i) % peers) for i in range(peers)])


def swapped(array):
    return moved(array, "in", lambda i: i ^ 1)


def pulled(rows, others, starts, pair, out_types, scale, shift):
    height, width = rows[0].shape
    n_rows, n_others, n_starts = len(rows), len(others), len(starts)

    def kernel(scale_ref, shift_ref, *refs):
        row_refs = refs[:n_rows]
        other_refs = refs[n_rows : n_rows + n_others]
        start_refs = refs[n_rows + n_others : n_rows + n_others + n_starts]
        out_refs = refs[n_rows + n_others + n_starts :]
        scale_now, shift_now = scale_ref[0], shift_ref[0]
        left = jnp.concatenate([ref[...] for ref in row_refs], axis=0)
        right = jnp.concatenate([ref[...] for ref in other_refs], axis=0)
        logits = lax.dot_general(
            left, right, (((1,), (1,)), ((), ())), preferred_element_type=jnp.float32
        )
        slope = jax.nn.sigmoid(scale_now * logits + shift_now)
        if pair is not None:
            row_ids = lax.broadcasted_iota(jnp.int32, slope.shape, 0)
            col_ids = lax.broadcasted_iota(jnp.int32, slope.shape, 1)
            matched = (col_ids - row_ids == (pair[1] - pair[0]) * height) & (
                row_ids // height == pair[0]
            )
            slope = slope - matched.astype(jnp.float32)
        weights = (scale_now * slope).astype(jnp.bfloat16)
        terms = jnp.dot(weights, right, preferred_element_type=jnp.float32)
        for i, out_ref in enumerate(out_refs):
            term = terms[i * height : (i + 1) * height]
            if n_starts:
                term = term + start_refs[i][...]
            out_ref[...] = term.astype(out_ref.dtype)

    vmem = pl.BlockSpec(memory_space=pltpu.VMEM)
    smem = pl.BlockSpec(memory_space=pltpu.SMEM)
    flops = 4 * height * height * width * n_rows * n_others
    return pl.pallas_call(
        kernel,
        out_shape=[jax.ShapeDtypeStruct((height, width), t) for t in out_types],
        in_specs=[smem, smem] + [vmem] * (n_rows + n_others + n_starts),
        out_specs=[vmem] * n_rows,
        cost_estimate=pl.CostEstimate(flops=flops, bytes_accessed=0, transcendentals=0),
    )(scale, shift, *rows, *others, *starts)


def shards(images, texts, scale, shift):
    chips = lax.axis_size("in") // CORES
    f32, bf16 = jnp.float32, jnp.bfloat16

    back_texts = moved(texts, "grp", lambda i: i + 1)
    near_images = [moved(images, "in", lambda i, k=k: i - CORES * k) for k in range(1, chips)]
    core_images, core_texts = swapped(images), swapped(texts)
    far_images = [swapped(block) for block in near_images]
    far_texts = swapped(back_texts)

    rows = [images] + near_images
    starts = pulled(
        rows, [texts, core_texts], [], (0, 0), [f32] * chips, scale, shift
    )
    text_total, sent_texts = pulled(
        [texts, back_texts],
        [images, core_images] + near_images + far_images,
        [],
        (0, 0),
        [f32, bf16],
        scale,
        shift,
    )
    sent_texts = moved(sent_texts, "grp", lambda i: i - 1)
    image_total, *sent_images = pulled(
        rows, [back_texts, far_texts], starts, None, [f32] + [bf16] * (chips - 1), scale, shift
    )
    for k, block in enumerate(sent_images, 1):
        image_total = image_total + moved(block, "in", lambda i, k=k: i + CORES * k).astype(f32)
    text_total = text_total + sent_texts.astype(f32)
    return image_total.astype(bf16), text_total.astype(bf16)


def solution(mesh):
    rows = P(("grp", "in"), None)
    return jax.shard_map(
        shards,
        mesh=mesh,
        in_specs=(rows, rows, P(), P()),
        out_specs=(rows, rows),
        check_vma=False,
    )
```

```python
import jax
import jax.numpy as jnp
from jax import lax
from jax.experimental import pallas as pl
from jax.experimental.pallas import tpu as pltpu
from jax.sharding import PartitionSpec as P

CORES = 2
VMEM = pl.BlockSpec(memory_space=pltpu.VMEM)
SMEM = pl.BlockSpec(memory_space=pltpu.SMEM)


def moved(array, axis, target):
    peers = lax.axis_size(axis)
    return lax.ppermute(array, axis, [(i, target(i) % peers) for i in range(peers)])


def swapped(array):
    return moved(array, "in", lambda i: i ^ 1)


def held(arrays, scale, shift):
    def kernel(scale_ref, shift_ref, *refs):
        sources, targets, sems = refs[: len(arrays)], refs[len(arrays) : -1], refs[-1]
        copies = [
            pltpu.make_async_copy(source, target, sems.at[i])
            for i, (source, target) in enumerate(zip(sources, targets))
        ]
        for copy in copies:
            copy.start()
        for copy in copies:
            copy.wait()

    return pl.pallas_call(
        kernel,
        out_shape=[jax.ShapeDtypeStruct(a.shape, a.dtype) for a in arrays],
        in_specs=[SMEM] * 2 + [pl.BlockSpec(memory_space=pl.ANY)] * len(arrays),
        out_specs=[VMEM] * len(arrays),
        scratch_shapes=[pltpu.SemaphoreType.DMA((len(arrays),))],
        compiler_params=pltpu.CompilerParams(vmem_limit_bytes=4 << 20),
    )(scale, shift, *arrays)


def pulled(jobs, out_types, scale, shift):
    height, width = jobs[0][0][0].shape
    arrays = [a for rows, others, starts, _ in jobs for a in (*rows, *others, *starts)]

    def kernel(scale_ref, shift_ref, *refs):
        in_refs, out_refs = iter(refs[: len(arrays)]), iter(refs[len(arrays) :])
        scale_now, shift_now = scale_ref[0], shift_ref[0]
        for rows, others, starts, paired in jobs:
            row_refs = [next(in_refs) for _ in rows]
            other_refs = [next(in_refs) for _ in others]
            start_refs = [next(in_refs) for _ in starts]
            left = jnp.concatenate([ref[...] for ref in row_refs], axis=0)
            right = jnp.concatenate([ref[...] for ref in other_refs], axis=0)
            logits = lax.dot_general(
                left, right, (((1,), (1,)), ((), ())), preferred_element_type=jnp.float32
            )
            slope = jax.nn.sigmoid(scale_now * logits + shift_now)
            if paired:
                row_ids = lax.broadcasted_iota(jnp.int32, slope.shape, 0)
                col_ids = lax.broadcasted_iota(jnp.int32, slope.shape, 1)
                matched = (col_ids == row_ids) & (row_ids < height)
                slope = slope - matched.astype(jnp.float32)
            weights = (scale_now * slope).astype(jnp.bfloat16)
            terms = jnp.dot(weights, right, preferred_element_type=jnp.float32)
            for i in range(len(rows)):
                term = terms[i * height : (i + 1) * height]
                if starts:
                    term = term + start_refs[i][...]
                out_ref = next(out_refs)
                out_ref[...] = term.astype(out_ref.dtype)

    pairs = sum(height * height * len(rows) * len(others) for rows, others, _, _ in jobs)
    size = sum(a.size * a.dtype.itemsize for a in arrays)
    size += sum(height * width * jnp.dtype(t).itemsize for t in out_types)
    return pl.pallas_call(
        kernel,
        out_shape=[jax.ShapeDtypeStruct((height, width), t) for t in out_types],
        in_specs=[SMEM] * 2 + [VMEM] * len(arrays),
        out_specs=[VMEM] * len(out_types),
        cost_estimate=pl.CostEstimate(
            flops=4 * pairs * width, bytes_accessed=size, transcendentals=pairs
        ),
        compiler_params=pltpu.CompilerParams(vmem_limit_bytes=2 * size + 16 * pairs + (4 << 20)),
    )(scale, shift, *arrays)


def summed(sums):
    shape = sums[0][0].shape
    arrays = [a for blocks in sums for a in blocks]

    def kernel(*refs):
        in_refs, out_refs = iter(refs[: len(arrays)]), refs[len(arrays) :]
        for blocks, out_ref in zip(sums, out_refs):
            total = next(in_refs)[...]
            for _ in blocks[1:]:
                total = total + next(in_refs)[...].astype(jnp.float32)
            out_ref[...] = total.astype(out_ref.dtype)

    size = sum(a.size * a.dtype.itemsize for a in arrays)
    return pl.pallas_call(
        kernel,
        out_shape=[jax.ShapeDtypeStruct(shape, jnp.bfloat16) for _ in sums],
        in_specs=[VMEM] * len(arrays),
        out_specs=[VMEM] * len(sums),
        cost_estimate=pl.CostEstimate(flops=size, bytes_accessed=size, transcendentals=0),
        compiler_params=pltpu.CompilerParams(vmem_limit_bytes=2 * size + (4 << 20)),
    )(*arrays)


def finished(first, second, second_extra):
    shape, dtype = first.shape, first.dtype

    def kernel(first_ref, second_ref, extra_ref, image_ref, text_ref, rounded_ref, sems):
        is_image_core = lax.rem(lax.axis_index("in"), CORES) == 0

        def to_images(source):
            return pltpu.make_async_copy(source, image_ref, sems.at[0])

        def to_texts(source):
            return pltpu.make_async_copy(source, text_ref, sems.at[1])

        @pl.when(is_image_core)
        def _():
            to_images(first_ref).start()

        @pl.when(jnp.logical_not(is_image_core))
        def _():
            to_texts(first_ref).start()

        total = second_ref[...] + extra_ref[...].astype(jnp.float32)
        rounded_ref[...] = total.astype(dtype)

        @pl.when(is_image_core)
        def _():
            to_texts(rounded_ref).start()

        @pl.when(jnp.logical_not(is_image_core))
        def _():
            to_images(rounded_ref).start()

        to_images(first_ref).wait()
        to_texts(first_ref).wait()

    size = 3 * first.size * 4
    return pl.pallas_call(
        kernel,
        out_shape=[jax.ShapeDtypeStruct(shape, dtype)] * 2,
        in_specs=[VMEM] * 3,
        out_specs=[pl.BlockSpec(memory_space=pl.ANY)] * 2,
        scratch_shapes=[pltpu.VMEM(shape, dtype), pltpu.SemaphoreType.DMA((2,))],
        cost_estimate=pl.CostEstimate(flops=size, bytes_accessed=size, transcendentals=0),
        compiler_params=pltpu.CompilerParams(vmem_limit_bytes=2 * size + (4 << 20)),
    )(first, second, second_extra)


def by_roles(images, texts, scale, shift):
    groups, members = lax.axis_size("grp"), lax.axis_size("in")
    f32, bf16 = jnp.float32, jnp.bfloat16

    def sent(array, target):
        pairs = []
        for group in range(groups):
            for chip in range(members // CORES):
                for core in range(CORES):
                    to_group, to_chip, to_core = target(group, chip, core)
                    pairs.append(
                        (
                            group * members + chip * CORES + core,
                            to_group % groups * members + (to_chip % 2) * CORES + to_core,
                        )
                    )
        return lax.ppermute(array, ("grp", "in"), pairs)

    is_image_core = lax.rem(lax.axis_index("in"), CORES) == 0
    first = jnp.where(is_image_core, images, texts)
    second = jnp.where(is_image_core, texts, images)
    got_a = sent(first, lambda g, x, c: (g, x + 1, 1) if c == 0 else (g + 1, x, 0))
    got_b = sent(second, lambda g, x, c: (g + 1, x, 0) if c == 0 else (g, x + 1, 1))
    other_first, other_second = swapped(first), swapped(second)
    starts = pulled(
        [
            ([first], [second, other_first], [], True),
            ([second], [first, other_second], [], True),
        ],
        [f32, f32],
        scale,
        shift,
    )
    swap_a = swapped(got_a)
    got_b, *starts = lax.optimization_barrier((got_b, *starts))
    swap_b = swapped(got_b)
    [back_a] = pulled(
        [([swap_a], [second, other_first, got_a, got_b], [], False)], [bf16], scale, shift
    )
    [back_b] = pulled(
        [([swap_b], [second, other_first, got_a, got_b], [], False)], [bf16], scale, shift
    )
    home_a = sent(back_a, lambda g, x, c: (g, x + 1, 0) if c == 0 else (g - 1, x, 1))
    home_b = sent(back_b, lambda g, x, c: (g, x + 1, 1) if c == 0 else (g - 1, x, 0))
    first_total, second_total = pulled(
        [
            ([first], [got_a, got_b], starts[:1], False),
            ([second], [swap_a, swap_b], starts[1:], False),
        ],
        [f32, f32],
        scale,
        shift,
    )
    [first_total] = summed([[first_total, home_a]])
    return tuple(finished(first_total, second_total, home_b))


def by_arrays(images, texts, scale, shift):
    chips = lax.axis_size("in") // CORES
    f32, bf16 = jnp.float32, jnp.bfloat16
    back_texts = moved(texts, "grp", lambda i: i + 1)
    near_images = [moved(images, "in", lambda i, k=k: i - CORES * k) for k in range(1, chips)]
    images, texts = held([images, texts], scale, shift)
    core_images, core_texts = swapped(images), swapped(texts)
    far_images = [swapped(block) for block in near_images]
    far_texts = swapped(back_texts)
    own_texts = [texts, core_texts]
    group_images = [images, core_images] + near_images + far_images

    starts = pulled(
        [(near_images, own_texts, [], False)], [f32] * (chips - 1), scale, shift
    )
    [sent_texts] = pulled([([back_texts], group_images, [], False)], [bf16], scale, shift)
    sent_images = pulled(
        [(near_images, [back_texts, far_texts], starts, False)],
        [bf16] * (chips - 1),
        scale,
        shift,
    )
    sent_texts, *sent_images = lax.optimization_barrier((sent_texts, *sent_images))
    sent_images = [
        moved(block, "in", lambda i, k=k: i + CORES * k) for k, block in enumerate(sent_images, 1)
    ]
    sent_texts = moved(sent_texts, "grp", lambda i: i - 1)
    image_total, text_total = pulled(
        [
            ([images], own_texts + [back_texts, far_texts], [], True),
            ([texts], group_images, [], True),
        ],
        [f32, f32],
        scale,
        shift,
    )
    return tuple(summed([[image_total] + sent_images, [text_total, sent_texts]]))


def shards(images, texts, scale, shift):
    if lax.axis_size("in") == 2 * CORES:
        return by_roles(images, texts, scale, shift)
    return by_arrays(images, texts, scale, shift)


def solution(mesh):
    rows = P(("grp", "in"), None)
    return jax.shard_map(
        shards,
        mesh=mesh,
        in_specs=(rows, rows, P(), P()),
        out_specs=(rows, rows),
        check_vma=False,
    )
```

```python
import jax
import jax.numpy as jnp
from jax import lax
from jax.experimental import pallas as pl
from jax.experimental.pallas import tpu as pltpu
from jax.sharding import PartitionSpec as P

CORES = 2
VMEM = pl.BlockSpec(memory_space=pltpu.VMEM)
SMEM = pl.BlockSpec(memory_space=pltpu.SMEM)


def moved(array, axis, target):
    peers = lax.axis_size(axis)
    return lax.ppermute(array, axis, [(i, target(i) % peers) for i in range(peers)])


def swapped(array):
    return moved(array, "in", lambda i: i ^ 1)


def held(arrays, scale, shift):
    def kernel(scale_ref, shift_ref, *refs):
        sources, targets, sems = refs[: len(arrays)], refs[len(arrays) : -1], refs[-1]
        copies = [
            pltpu.make_async_copy(source, target, sems.at[i])
            for i, (source, target) in enumerate(zip(sources, targets))
        ]
        for copy in copies:
            copy.start()
        for copy in copies:
            copy.wait()

    return pl.pallas_call(
        kernel,
        out_shape=[jax.ShapeDtypeStruct(a.shape, a.dtype) for a in arrays],
        in_specs=[SMEM] * 2 + [pl.BlockSpec(memory_space=pl.ANY)] * len(arrays),
        out_specs=[VMEM] * len(arrays),
        scratch_shapes=[pltpu.SemaphoreType.DMA((len(arrays),))],
        compiler_params=pltpu.CompilerParams(vmem_limit_bytes=4 << 20),
    )(scale, shift, *arrays)


def pulled(jobs, out_types, scale, shift):
    height, width = jobs[0][0][0].shape
    arrays = [a for rows, others, starts, _ in jobs for a in (*rows, *others, *starts)]

    def kernel(scale_ref, shift_ref, *refs):
        in_refs, out_refs = iter(refs[: len(arrays)]), iter(refs[len(arrays) :])
        scale_now, shift_now = scale_ref[0], shift_ref[0]
        for rows, others, starts, paired in jobs:
            row_refs = [next(in_refs) for _ in rows]
            other_refs = [next(in_refs) for _ in others]
            start_refs = [next(in_refs) for _ in starts]
            left = jnp.concatenate([ref[...] for ref in row_refs], axis=0)
            right = jnp.concatenate([ref[...] for ref in other_refs], axis=0)
            logits = lax.dot_general(
                left, right, (((1,), (1,)), ((), ())), preferred_element_type=jnp.float32
            )
            slope = jax.nn.sigmoid(scale_now * logits + shift_now)
            if paired:
                row_ids = lax.broadcasted_iota(jnp.int32, slope.shape, 0)
                col_ids = lax.broadcasted_iota(jnp.int32, slope.shape, 1)
                matched = (col_ids == row_ids) & (row_ids < height)
                slope = slope - matched.astype(jnp.float32)
            weights = (scale_now * slope).astype(jnp.bfloat16)
            terms = jnp.dot(weights, right, preferred_element_type=jnp.float32)
            for i in range(len(rows)):
                term = terms[i * height : (i + 1) * height]
                if starts:
                    term = term + start_refs[i][...]
                out_ref = next(out_refs)
                out_ref[...] = term.astype(out_ref.dtype)

    pairs = sum(height * height * len(rows) * len(others) for rows, others, _, _ in jobs)
    size = sum(a.size * a.dtype.itemsize for a in arrays)
    size += sum(height * width * jnp.dtype(t).itemsize for t in out_types)
    return pl.pallas_call(
        kernel,
        out_shape=[jax.ShapeDtypeStruct((height, width), t) for t in out_types],
        in_specs=[SMEM] * 2 + [VMEM] * len(arrays),
        out_specs=[VMEM] * len(out_types),
        cost_estimate=pl.CostEstimate(
            flops=4 * pairs * width, bytes_accessed=size, transcendentals=pairs
        ),
        compiler_params=pltpu.CompilerParams(vmem_limit_bytes=2 * size + 16 * pairs + (4 << 20)),
    )(scale, shift, *arrays)


def summed(sums):
    shape = sums[0][0].shape
    arrays = [a for blocks in sums for a in blocks]

    def kernel(*refs):
        in_refs, out_refs = iter(refs[: len(arrays)]), refs[len(arrays) :]
        for blocks, out_ref in zip(sums, out_refs):
            total = next(in_refs)[...]
            for _ in blocks[1:]:
                total = total + next(in_refs)[...].astype(jnp.float32)
            out_ref[...] = total.astype(out_ref.dtype)

    size = sum(a.size * a.dtype.itemsize for a in arrays)
    return pl.pallas_call(
        kernel,
        out_shape=[jax.ShapeDtypeStruct(shape, jnp.bfloat16) for _ in sums],
        in_specs=[VMEM] * len(arrays),
        out_specs=[VMEM] * len(sums),
        cost_estimate=pl.CostEstimate(flops=size, bytes_accessed=size, transcendentals=0),
        compiler_params=pltpu.CompilerParams(vmem_limit_bytes=2 * size + (4 << 20)),
    )(*arrays)


def placed(total, extra, kept, texts_on):
    shape, dtype = total.shape, jnp.bfloat16
    pieces = 2
    rows = shape[0] // pieces

    def kernel(total_ref, extra_ref, *refs):
        image_ref, text_ref, rounded_ref, sems = refs[-4:]
        is_text = lax.rem(lax.axis_index("in"), CORES) == texts_on

        def copy(piece, target_ref):
            part = pl.ds(piece * rows, rows)
            return pltpu.make_async_copy(rounded_ref.at[part], target_ref.at[part], sems.at[piece])

        for piece in range(pieces):
            part = pl.ds(piece * rows, rows)
            block = total_ref[part, :] + extra_ref[part, :].astype(jnp.float32)
            rounded_ref[part, :] = block.astype(dtype)
            pl.when(is_text)(lambda piece=piece: copy(piece, text_ref).start())
            pl.when(jnp.logical_not(is_text))(lambda piece=piece: copy(piece, image_ref).start())
        for piece in range(pieces):
            copy(piece, image_ref).wait()

    hbm = pl.BlockSpec(memory_space=pl.ANY)
    kept = [] if kept is None else list(kept)
    size = total.size * 4
    return pl.pallas_call(
        kernel,
        out_shape=[jax.ShapeDtypeStruct(shape, dtype)] * 2,
        in_specs=[VMEM] * 2 + [hbm] * len(kept),
        out_specs=[hbm] * 2,
        scratch_shapes=[pltpu.VMEM(shape, dtype), pltpu.SemaphoreType.DMA((pieces,))],
        input_output_aliases={2 + i: i for i in range(len(kept))},
        cost_estimate=pl.CostEstimate(flops=size, bytes_accessed=size, transcendentals=0),
        compiler_params=pltpu.CompilerParams(vmem_limit_bytes=4 * size + (4 << 20)),
    )(total, extra, *kept)


def ranked(images, texts, scale, shift):
    def kernel(scale_ref, shift_ref, image_ref, text_ref, first_ref, second_ref, sems):
        def copy(number, source_ref):
            target_ref = (first_ref, second_ref)[number]
            return pltpu.make_async_copy(source_ref, target_ref, sems.at[number])

        core = lax.rem(lax.axis_index("in"), CORES)
        for number, sources in enumerate([(image_ref, text_ref), (text_ref, image_ref)]):

            @pl.when(core == number)
            def _(sources=sources):
                copy(0, sources[0]).start()
                copy(1, sources[1]).start()

        copy(0, image_ref).wait()
        copy(1, text_ref).wait()

    return pl.pallas_call(
        kernel,
        out_shape=[jax.ShapeDtypeStruct(images.shape, images.dtype)] * 2,
        in_specs=[SMEM] * 2 + [pl.BlockSpec(memory_space=pl.ANY)] * 2,
        out_specs=[VMEM] * 2,
        scratch_shapes=[pltpu.SemaphoreType.DMA((2,))],
        compiler_params=pltpu.CompilerParams(vmem_limit_bytes=4 << 20),
    )(scale, shift, *[pltpu.with_memory_space_constraint(a, pltpu.HBM) for a in (images, texts)])


def by_roles(images, texts, scale, shift):
    groups, members = lax.axis_size("grp"), lax.axis_size("in")
    f32, bf16 = jnp.float32, jnp.bfloat16

    def sent(array, target):
        pairs = []
        for group in range(groups):
            for chip in range(members // CORES):
                for core in range(CORES):
                    to_group, to_chip, to_core = target(group, chip, core)
                    pairs.append(
                        (
                            group * members + chip * CORES + core,
                            to_group % groups * members + (to_chip % 2) * CORES + to_core,
                        )
                    )
        return lax.ppermute(array, ("grp", "in"), pairs)

    is_image_core = lax.rem(lax.axis_index("in"), CORES) == 0
    got_texts = sent(texts, lambda g, x, c: (g, x, 1) if c == 0 else (g + 1, x, 0))
    got_images = sent(images, lambda g, x, c: (g, x + 1, 1) if c == 0 else (g, x, 0))
    first, second = ranked(images, texts, scale, shift)
    got_b = sent(second, lambda g, x, c: (g + 1, x, 0) if c == 0 else (g, x + 1, 1))
    got_a = jnp.where(is_image_core, got_texts, got_images)
    other_second = jnp.where(is_image_core, got_images, got_texts)
    got_a, first_again = lax.optimization_barrier((got_a, first))
    swap_a = swapped(got_a)
    other_first = swapped(first_again)
    swap_b = swapped(got_b)
    [back_a] = pulled(
        [([swap_a], [second, other_first, got_a, got_b], [], False)], [bf16], scale, shift
    )
    [back_b] = pulled(
        [([swap_b], [second, other_first, got_a, got_b], [], False)], [bf16], scale, shift
    )
    home_a = sent(back_a, lambda g, x, c: (g, x + 1, 0) if c == 0 else (g - 1, x, 1))
    home_b = sent(back_b, lambda g, x, c: (g, x + 1, 1) if c == 0 else (g - 1, x, 0))
    first_total, second_total = pulled(
        [
            ([first], [second, other_first, got_a, got_b], [], True),
            ([second], [first, other_second, swap_a, swap_b], [], True),
        ],
        [f32, f32],
        scale,
        shift,
    )
    outputs = placed(first_total, home_a, None, 1)
    return tuple(placed(second_total, home_b, outputs, 0))


def by_arrays(images, texts, scale, shift):
    chips = lax.axis_size("in") // CORES
    f32, bf16 = jnp.float32, jnp.bfloat16
    back_texts = moved(texts, "grp", lambda i: i + 1)
    near_images = [moved(images, "in", lambda i, k=k: i - CORES * k) for k in range(1, chips)]
    images, texts = held([images, texts], scale, shift)
    core_images, core_texts = swapped(images), swapped(texts)
    far_images = [swapped(block) for block in near_images]
    far_texts = swapped(back_texts)
    own_texts = [texts, core_texts]
    group_images = [images, core_images] + near_images + far_images

    starts = pulled(
        [(near_images, own_texts, [], False)], [f32] * (chips - 1), scale, shift
    )
    [sent_texts] = pulled([([back_texts], group_images, [], False)], [bf16], scale, shift)
    sent_images = pulled(
        [(near_images, [back_texts, far_texts], starts, False)],
        [bf16] * (chips - 1),
        scale,
        shift,
    )
    sent_texts, *sent_images = lax.optimization_barrier((sent_texts, *sent_images))
    sent_images = [
        moved(block, "in", lambda i, k=k: i + CORES * k) for k, block in enumerate(sent_images, 1)
    ]
    sent_texts = moved(sent_texts, "grp", lambda i: i - 1)
    image_total, text_total = pulled(
        [
            ([images], own_texts + [back_texts, far_texts], [], True),
            ([texts], group_images, [], True),
        ],
        [f32, f32],
        scale,
        shift,
    )
    return tuple(summed([[image_total] + sent_images, [text_total, sent_texts]]))


def shards(images, texts, scale, shift):
    if lax.axis_size("in") == 2 * CORES:
        return by_roles(images, texts, scale, shift)
    return by_arrays(images, texts, scale, shift)


def solution(mesh):
    rows = P(("grp", "in"), None)
    return jax.shard_map(
        shards,
        mesh=mesh,
        in_specs=(rows, rows, P(), P()),
        out_specs=(rows, rows),
        check_vma=False,
    )
```

```python
import jax
import jax.numpy as jnp
from jax import lax
from jax.experimental import pallas as pl
from jax.experimental.pallas import tpu as pltpu
from jax.sharding import PartitionSpec as P

CORES = 2
VMEM = pl.BlockSpec(memory_space=pltpu.VMEM)
SMEM = pl.BlockSpec(memory_space=pltpu.SMEM)


def moved(array, axis, target):
    peers = lax.axis_size(axis)
    return lax.ppermute(array, axis, [(i, target(i) % peers) for i in range(peers)])


def swapped(array):
    return moved(array, "in", lambda i: i ^ 1)


def held(arrays, scale, shift):
    def kernel(scale_ref, shift_ref, *refs):
        sources, targets, sems = refs[: len(arrays)], refs[len(arrays) : -1], refs[-1]
        copies = [
            pltpu.make_async_copy(source, target, sems.at[i])
            for i, (source, target) in enumerate(zip(sources, targets))
        ]
        for copy in copies:
            copy.start()
        for copy in copies:
            copy.wait()

    return pl.pallas_call(
        kernel,
        out_shape=[jax.ShapeDtypeStruct(a.shape, a.dtype) for a in arrays],
        in_specs=[SMEM] * 2 + [pl.BlockSpec(memory_space=pl.ANY)] * len(arrays),
        out_specs=[VMEM] * len(arrays),
        scratch_shapes=[pltpu.SemaphoreType.DMA((len(arrays),))],
        compiler_params=pltpu.CompilerParams(vmem_limit_bytes=4 << 20),
    )(scale, shift, *arrays)


def pulled(jobs, out_types, scale, shift, only=None, into=None):
    height, width = jobs[0][0][0].shape
    kept = [] if into is None else [into]
    arrays = [a for rows, others, starts, _ in jobs for a in (*rows, *others, *starts)]

    scalars = [scale] if shift is None else [scale, shift]

    def kernel(*refs):
        scalar_refs, refs = refs[: len(scalars)], refs[len(scalars) :]

        def run():
            if shift is None:
                values = scalar_refs[0][0:1, 0:1], scalar_refs[0][1:2, 0:1]
            else:
                values = scalar_refs[0][0], scalar_refs[1][0]
            write(*values, refs[: len(arrays)], refs[len(arrays) + len(kept) :])

        if only is None:
            run()
        else:
            here = lax.rem(lax.axis_index("in"), CORES) == only
            pl.when(here)(run)

        if kept:

            @pl.when(jnp.logical_not(here))
            def _():
                refs[-1][...] = refs[-2][...]

    def write(scale_now, shift_now, in_refs, out_refs):
        in_refs, out_refs = iter(in_refs), iter(out_refs)
        for rows, others, starts, paired in jobs:
            row_refs = [next(in_refs) for _ in rows]
            other_refs = [next(in_refs) for _ in others]
            start_refs = [next(in_refs) for _ in starts]
            left = jnp.concatenate([ref[...] for ref in row_refs], axis=0)
            right = jnp.concatenate([ref[...] for ref in other_refs], axis=0)
            logits = lax.dot_general(
                left, right, (((1,), (1,)), ((), ())), preferred_element_type=jnp.float32
            )
            slope = jax.nn.sigmoid(scale_now * logits + shift_now)
            if paired:
                row_ids = lax.broadcasted_iota(jnp.int32, slope.shape, 0)
                col_ids = lax.broadcasted_iota(jnp.int32, slope.shape, 1)
                matched = (col_ids == row_ids) & (row_ids < height)
                slope = slope - matched.astype(jnp.float32)
            weights = (scale_now * slope).astype(jnp.bfloat16)
            terms = jnp.dot(weights, right, preferred_element_type=jnp.float32)
            for i in range(len(rows)):
                term = terms[i * height : (i + 1) * height]
                if starts:
                    term = term + start_refs[i][...]
                out_ref = next(out_refs)
                out_ref[...] = term.astype(out_ref.dtype)

    pairs = sum(height * height * len(rows) * len(others) for rows, others, _, _ in jobs)
    size = sum(a.size * a.dtype.itemsize for a in arrays)
    size += sum(height * width * jnp.dtype(t).itemsize for t in out_types)
    return pl.pallas_call(
        kernel,
        out_shape=[jax.ShapeDtypeStruct((height, width), t) for t in out_types],
        in_specs=[VMEM if shift is None else SMEM] * len(scalars)
        + [VMEM] * (len(arrays) + len(kept)),
        out_specs=[VMEM] * len(out_types),
        cost_estimate=pl.CostEstimate(
            flops=4 * pairs * width, bytes_accessed=size, transcendentals=pairs
        ),
        compiler_params=pltpu.CompilerParams(vmem_limit_bytes=2 * size + 16 * pairs + (4 << 20)),
    )(*scalars, *arrays, *kept)


def summed(sums):
    shape = sums[0][0].shape
    arrays = [a for blocks in sums for a in blocks]

    def kernel(*refs):
        in_refs, out_refs = iter(refs[: len(arrays)]), refs[len(arrays) :]
        for blocks, out_ref in zip(sums, out_refs):
            total = next(in_refs)[...]
            for _ in blocks[1:]:
                total = total + next(in_refs)[...].astype(jnp.float32)
            out_ref[...] = total.astype(out_ref.dtype)

    size = sum(a.size * a.dtype.itemsize for a in arrays)
    return pl.pallas_call(
        kernel,
        out_shape=[jax.ShapeDtypeStruct(shape, jnp.bfloat16) for _ in sums],
        in_specs=[VMEM] * len(arrays),
        out_specs=[VMEM] * len(sums),
        cost_estimate=pl.CostEstimate(flops=size, bytes_accessed=size, transcendentals=0),
        compiler_params=pltpu.CompilerParams(vmem_limit_bytes=2 * size + (4 << 20)),
    )(*arrays)


def placed(total, extra, kept, texts_on):
    shape, dtype = total.shape, jnp.bfloat16
    pieces = 2
    rows = shape[0] // pieces

    def kernel(total_ref, extra_ref, *refs):
        image_ref, text_ref, rounded_ref, sems = refs[-4:]
        is_text = lax.rem(lax.axis_index("in"), CORES) == texts_on

        def copy(piece, target_ref):
            part = pl.ds(piece * rows, rows)
            return pltpu.make_async_copy(rounded_ref.at[part], target_ref.at[part], sems.at[piece])

        for piece in range(pieces):
            part = pl.ds(piece * rows, rows)
            block = total_ref[part, :] + extra_ref[part, :].astype(jnp.float32)
            rounded_ref[part, :] = block.astype(dtype)
            pl.when(is_text)(lambda piece=piece: copy(piece, text_ref).start())
            pl.when(jnp.logical_not(is_text))(lambda piece=piece: copy(piece, image_ref).start())
        for piece in range(pieces):
            copy(piece, image_ref).wait()

    hbm = pl.BlockSpec(memory_space=pl.ANY)
    kept = [] if kept is None else list(kept)
    size = total.size * 4
    return pl.pallas_call(
        kernel,
        out_shape=[jax.ShapeDtypeStruct(shape, dtype)] * 2,
        in_specs=[VMEM] * 2 + [hbm] * len(kept),
        out_specs=[hbm] * 2,
        scratch_shapes=[pltpu.VMEM(shape, dtype), pltpu.SemaphoreType.DMA((pieces,))],
        input_output_aliases={2 + i: i for i in range(len(kept))},
        cost_estimate=pl.CostEstimate(flops=size, bytes_accessed=size, transcendentals=0),
        compiler_params=pltpu.CompilerParams(vmem_limit_bytes=4 * size + (4 << 20)),
    )(total, extra, *kept)


def opened():
    def kernel(out_ref):
        out_ref[...] = jnp.zeros_like(out_ref)

    return pl.pallas_call(
        kernel,
        out_shape=jax.ShapeDtypeStruct((8, 128), jnp.float32),
        out_specs=VMEM,
        cost_estimate=pl.CostEstimate(flops=10**10, bytes_accessed=2**26, transcendentals=0),
        compiler_params=pltpu.CompilerParams(vmem_limit_bytes=1 << 20),
    )()


def ranked(images, texts, opening):
    def kernel(image_ref, text_ref, opening_ref, first_ref, second_ref):
        core = lax.rem(lax.axis_index("in"), CORES)
        for number, sources in enumerate([(image_ref, text_ref), (text_ref, image_ref)]):

            @pl.when(core == number)
            def _(sources=sources):
                first_ref[...] = sources[0][...]
                second_ref[...] = sources[1][...]

    return pl.pallas_call(
        kernel,
        out_shape=[jax.ShapeDtypeStruct(images.shape, images.dtype)] * 2,
        in_specs=[VMEM] * 3,
        out_specs=[VMEM] * 2,
        compiler_params=pltpu.CompilerParams(vmem_limit_bytes=4 << 20),
    )(images, texts, opening)


def packed(scale, shift):
    def kernel(scale_ref, shift_ref, out_ref):
        out_ref[0:1, :] = jnp.full((1, 128), scale_ref[0], jnp.float32)
        out_ref[1:2, :] = jnp.full((1, 128), shift_ref[0], jnp.float32)

    return pl.pallas_call(
        kernel,
        out_shape=jax.ShapeDtypeStruct((2, 128), jnp.float32),
        in_specs=[SMEM] * 2,
        out_specs=VMEM,
        compiler_params=pltpu.CompilerParams(vmem_limit_bytes=1 << 20),
    )(scale, shift)


def by_roles(images, texts, scale, shift):
    groups, members = lax.axis_size("grp"), lax.axis_size("in")
    f32, bf16 = jnp.float32, jnp.bfloat16

    def sent(array, target):
        pairs = []
        for group in range(groups):
            for chip in range(members // CORES):
                for core in range(CORES):
                    to_group, to_chip, to_core = target(group, chip, core)
                    pairs.append(
                        (
                            group * members + chip * CORES + core,
                            to_group % groups * members + (to_chip % 2) * CORES + to_core,
                        )
                    )
        return lax.ppermute(array, ("grp", "in"), pairs)

    is_image_core = lax.rem(lax.axis_index("in"), CORES) == 0
    other_images, other_texts = swapped(images), swapped(texts)
    first, second = ranked(images, texts, opened())
    other_first = jnp.where(is_image_core, other_texts, other_images)
    other_second = jnp.where(is_image_core, other_images, other_texts)
    got_a, got_b = [
        sent(block, lambda g, x, c: (g, x + 1, 1) if c == 0 else (g + 1, x, 0))
        for block in (first, other_second)
    ]
    starts = pulled(
        [
            ([first], [second, other_first], [], True),
            ([second], [first, other_second], [], True),
        ],
        [f32, f32],
        scale,
        shift,
    )
    got_a, both = lax.optimization_barrier((got_a, packed(scale, shift)))
    swap_a = swapped(got_a)
    got_b, *starts = lax.optimization_barrier((got_b, *starts))
    job_a = [([swap_a], [second, other_first, got_a, got_b], [], False)]
    [back_a] = pulled(job_a, [bf16], scale, shift, 1)
    got_b_again, back_a = lax.optimization_barrier((got_b, back_a))
    swap_b = swapped(got_b_again)
    [back_a] = pulled(job_a, [bf16], scale, shift, 0, back_a)
    [back_b] = pulled(
        [([swap_b], [second, other_first, got_a, got_b], [], False)], [bf16], scale, shift
    )
    home_a = sent(back_a, lambda g, x, c: (g, x + 1, 0) if c == 0 else (g - 1, x, 1))
    home_b = sent(back_b, lambda g, x, c: (g, x + 1, 1) if c == 0 else (g - 1, x, 0))
    first_total, second_total = pulled(
        [
            ([first], [got_a, got_b], starts[:1], False),
            ([second], [swap_a, swap_b], starts[1:], False),
        ],
        [f32, f32],
        both,
        None,
    )
    outputs = placed(first_total, home_a, None, 1)
    return tuple(placed(second_total, home_b, outputs, 0))


def by_arrays(images, texts, scale, shift):
    chips = lax.axis_size("in") // CORES
    f32, bf16 = jnp.float32, jnp.bfloat16
    back_texts = moved(texts, "grp", lambda i: i + 1)
    near_images = [moved(images, "in", lambda i, k=k: i - CORES * k) for k in range(1, chips)]
    images, texts = held([images, texts], scale, shift)
    core_images, core_texts = swapped(images), swapped(texts)
    far_images = [swapped(block) for block in near_images]
    far_texts = swapped(back_texts)
    own_texts = [texts, core_texts]
    group_images = [images, core_images] + near_images + far_images

    starts = pulled(
        [(near_images, own_texts, [], False)], [f32] * (chips - 1), scale, shift
    )
    [sent_texts] = pulled([([back_texts], group_images, [], False)], [bf16], scale, shift)
    sent_images = pulled(
        [(near_images, [back_texts, far_texts], starts, False)],
        [bf16] * (chips - 1),
        scale,
        shift,
    )
    sent_texts, *sent_images = lax.optimization_barrier((sent_texts, *sent_images))
    sent_images = [
        moved(block, "in", lambda i, k=k: i + CORES * k) for k, block in enumerate(sent_images, 1)
    ]
    sent_texts = moved(sent_texts, "grp", lambda i: i - 1)
    image_total, text_total = pulled(
        [
            ([images], own_texts + [back_texts, far_texts], [], True),
            ([texts], group_images, [], True),
        ],
        [f32, f32],
        scale,
        shift,
    )
    return tuple(summed([[image_total] + sent_images, [text_total, sent_texts]]))


def shards(images, texts, scale, shift):
    if lax.axis_size("in") == 2 * CORES:
        return by_roles(images, texts, scale, shift)
    return by_arrays(images, texts, scale, shift)


def solution(mesh):
    rows = P(("grp", "in"), None)
    return jax.shard_map(
        shards,
        mesh=mesh,
        in_specs=(rows, rows, P(), P()),
        out_specs=(rows, rows),
        check_vma=False,
    )
```

```python
import jax
import jax.numpy as jnp
from jax import lax
from jax.experimental import pallas as pl
from jax.experimental.pallas import tpu as pltpu
from jax.sharding import PartitionSpec as P

CORES = 2
VMEM = pl.BlockSpec(memory_space=pltpu.VMEM)
SMEM = pl.BlockSpec(memory_space=pltpu.SMEM)


def moved(array, axis, target):
    peers = lax.axis_size(axis)
    return lax.ppermute(array, axis, [(i, target(i) % peers) for i in range(peers)])


def swapped(array):
    return moved(array, "in", lambda i: i ^ 1)


def held(arrays, scale, shift):
    def kernel(scale_ref, shift_ref, *refs):
        sources, targets, sems = refs[: len(arrays)], refs[len(arrays) : -1], refs[-1]
        copies = [
            pltpu.make_async_copy(source, target, sems.at[i])
            for i, (source, target) in enumerate(zip(sources, targets))
        ]
        for copy in copies:
            copy.start()
        for copy in copies:
            copy.wait()

    return pl.pallas_call(
        kernel,
        out_shape=[jax.ShapeDtypeStruct(a.shape, a.dtype) for a in arrays],
        in_specs=[SMEM] * 2 + [pl.BlockSpec(memory_space=pl.ANY)] * len(arrays),
        out_specs=[VMEM] * len(arrays),
        scratch_shapes=[pltpu.SemaphoreType.DMA((len(arrays),))],
        compiler_params=pltpu.CompilerParams(vmem_limit_bytes=4 << 20),
    )(scale, shift, *arrays)


def pulled(jobs, out_types, scale, shift, only=None, into=None):
    height, width = jobs[0][0][0].shape
    kept = [] if into is None else [into]
    arrays = [a for rows, others, starts, _ in jobs for a in (*rows, *others, *starts)]

    scalars = [scale] if shift is None else [scale, shift]

    def kernel(*refs):
        scalar_refs, refs = refs[: len(scalars)], refs[len(scalars) :]

        def run():
            if shift is None:
                values = scalar_refs[0][0:1, 0:1], scalar_refs[0][1:2, 0:1]
            else:
                values = scalar_refs[0][0], scalar_refs[1][0]
            write(*values, refs[: len(arrays)], refs[len(arrays) + len(kept) :])

        if only is None:
            run()
        else:
            here = lax.rem(lax.axis_index("in"), CORES) == only
            pl.when(here)(run)

        if kept:

            @pl.when(jnp.logical_not(here))
            def _():
                refs[-1][...] = refs[-2][...]

    def write(scale_now, shift_now, in_refs, out_refs):
        in_refs, out_refs = iter(in_refs), iter(out_refs)
        for rows, others, starts, paired in jobs:
            row_refs = [next(in_refs) for _ in rows]
            other_refs = [next(in_refs) for _ in others]
            start_refs = [next(in_refs) for _ in starts]
            left = jnp.concatenate([ref[...] for ref in row_refs], axis=0)
            right = jnp.concatenate([ref[...] for ref in other_refs], axis=0)
            logits = lax.dot_general(
                left, right, (((1,), (1,)), ((), ())), preferred_element_type=jnp.float32
            )
            slope = jax.nn.sigmoid(scale_now * logits + shift_now)
            if paired:
                row_ids = lax.broadcasted_iota(jnp.int32, slope.shape, 0)
                col_ids = lax.broadcasted_iota(jnp.int32, slope.shape, 1)
                matched = (col_ids == row_ids) & (row_ids < height)
                slope = slope - matched.astype(jnp.float32)
            weights = (scale_now * slope).astype(jnp.bfloat16)
            terms = jnp.dot(weights, right, preferred_element_type=jnp.float32)
            for i in range(len(rows)):
                term = terms[i * height : (i + 1) * height]
                if starts:
                    term = term + start_refs[i][...]
                out_ref = next(out_refs)
                out_ref[...] = term.astype(out_ref.dtype)

    pairs = sum(height * height * len(rows) * len(others) for rows, others, _, _ in jobs)
    size = sum(a.size * a.dtype.itemsize for a in arrays)
    size += sum(height * width * jnp.dtype(t).itemsize for t in out_types)
    return pl.pallas_call(
        kernel,
        out_shape=[jax.ShapeDtypeStruct((height, width), t) for t in out_types],
        in_specs=[VMEM if shift is None else SMEM] * len(scalars)
        + [VMEM] * (len(arrays) + len(kept)),
        out_specs=[VMEM] * len(out_types),
        cost_estimate=pl.CostEstimate(
            flops=4 * pairs * width, bytes_accessed=size, transcendentals=pairs
        ),
        compiler_params=pltpu.CompilerParams(vmem_limit_bytes=2 * size + 16 * pairs + (4 << 20)),
    )(*scalars, *arrays, *kept)


def summed(sums):
    shape = sums[0][0].shape
    arrays = [a for blocks in sums for a in blocks]

    def kernel(*refs):
        in_refs, out_refs = iter(refs[: len(arrays)]), refs[len(arrays) :]
        for blocks, out_ref in zip(sums, out_refs):
            total = next(in_refs)[...]
            for _ in blocks[1:]:
                total = total + next(in_refs)[...].astype(jnp.float32)
            out_ref[...] = total.astype(out_ref.dtype)

    size = sum(a.size * a.dtype.itemsize for a in arrays)
    return pl.pallas_call(
        kernel,
        out_shape=[jax.ShapeDtypeStruct(shape, jnp.bfloat16) for _ in sums],
        in_specs=[VMEM] * len(arrays),
        out_specs=[VMEM] * len(sums),
        cost_estimate=pl.CostEstimate(flops=size, bytes_accessed=size, transcendentals=0),
        compiler_params=pltpu.CompilerParams(vmem_limit_bytes=2 * size + (4 << 20)),
    )(*arrays)


def placed(total, extra, kept, texts_on):
    shape, dtype = total.shape, jnp.bfloat16
    pieces = 2
    rows = shape[0] // pieces

    def kernel(total_ref, extra_ref, *refs):
        image_ref, text_ref, rounded_ref, sems = refs[-4:]
        is_text = lax.rem(lax.axis_index("in"), CORES) == texts_on

        def copy(piece, target_ref):
            part = pl.ds(piece * rows, rows)
            return pltpu.make_async_copy(rounded_ref.at[part], target_ref.at[part], sems.at[piece])

        for piece in range(pieces):
            part = pl.ds(piece * rows, rows)
            block = total_ref[part, :] + extra_ref[part, :].astype(jnp.float32)
            rounded_ref[part, :] = block.astype(dtype)
            pl.when(is_text)(lambda piece=piece: copy(piece, text_ref).start())
            pl.when(jnp.logical_not(is_text))(lambda piece=piece: copy(piece, image_ref).start())
        for piece in range(pieces):
            copy(piece, image_ref).wait()

    hbm = pl.BlockSpec(memory_space=pl.ANY)
    kept = [] if kept is None else list(kept)
    size = total.size * 4
    return pl.pallas_call(
        kernel,
        out_shape=[jax.ShapeDtypeStruct(shape, dtype)] * 2,
        in_specs=[VMEM] * 2 + [hbm] * len(kept),
        out_specs=[hbm] * 2,
        scratch_shapes=[pltpu.VMEM(shape, dtype), pltpu.SemaphoreType.DMA((pieces,))],
        input_output_aliases={2 + i: i for i in range(len(kept))},
        cost_estimate=pl.CostEstimate(flops=size, bytes_accessed=size, transcendentals=0),
        compiler_params=pltpu.CompilerParams(vmem_limit_bytes=4 * size + (4 << 20)),
    )(total, extra, *kept)


def opened():
    def kernel(out_ref):
        out_ref[...] = jnp.zeros_like(out_ref)

    return pl.pallas_call(
        kernel,
        out_shape=jax.ShapeDtypeStruct((8, 128), jnp.float32),
        out_specs=VMEM,
        cost_estimate=pl.CostEstimate(flops=10**10, bytes_accessed=2**26, transcendentals=0),
        compiler_params=pltpu.CompilerParams(vmem_limit_bytes=1 << 20),
    )()


def ranked(images, texts, opening):
    def kernel(image_ref, text_ref, opening_ref, first_ref, second_ref):
        core = lax.rem(lax.axis_index("in"), CORES)
        for number, sources in enumerate([(image_ref, text_ref), (text_ref, image_ref)]):

            @pl.when(core == number)
            def _(sources=sources):
                first_ref[...] = sources[0][...]
                second_ref[...] = sources[1][...]

    return pl.pallas_call(
        kernel,
        out_shape=[jax.ShapeDtypeStruct(images.shape, images.dtype)] * 2,
        in_specs=[VMEM] * 3,
        out_specs=[VMEM] * 2,
        compiler_params=pltpu.CompilerParams(vmem_limit_bytes=4 << 20),
    )(images, texts, opening)


def packed(scale, shift):
    def kernel(scale_ref, shift_ref, out_ref):
        out_ref[0:1, :] = jnp.full((1, 128), scale_ref[0], jnp.float32)
        out_ref[1:2, :] = jnp.full((1, 128), shift_ref[0], jnp.float32)

    return pl.pallas_call(
        kernel,
        out_shape=jax.ShapeDtypeStruct((2, 128), jnp.float32),
        in_specs=[SMEM] * 2,
        out_specs=VMEM,
        compiler_params=pltpu.CompilerParams(vmem_limit_bytes=1 << 20),
    )(scale, shift)


def by_roles(images, texts, scale, shift):
    groups, members = lax.axis_size("grp"), lax.axis_size("in")
    f32, bf16 = jnp.float32, jnp.bfloat16

    def sent(array, target):
        pairs = []
        for group in range(groups):
            for chip in range(members // CORES):
                for core in range(CORES):
                    to_group, to_chip, to_core = target(group, chip, core)
                    pairs.append(
                        (
                            group * members + chip * CORES + core,
                            to_group % groups * members + (to_chip % 2) * CORES + to_core,
                        )
                    )
        return lax.ppermute(array, ("grp", "in"), pairs)

    is_image_core = lax.rem(lax.axis_index("in"), CORES) == 0
    other_texts, other_images = swapped(texts), swapped(images)
    first, second = ranked(images, texts, opened())
    other_first = jnp.where(is_image_core, other_texts, other_images)
    other_second = jnp.where(is_image_core, other_images, other_texts)
    got_a, got_b = [
        sent(block, lambda g, x, c: (g, x + 1, 1) if c == 0 else (g + 1, x, 0))
        for block in (first, other_second)
    ]
    got_a, both = lax.optimization_barrier((got_a, packed(scale, shift)))
    swap_a = swapped(got_a)
    job_a = [([swap_a], [second, other_first, got_a, got_b], [], False)]
    [back_a] = pulled(job_a, [bf16], scale, shift, 1)
    got_b_again, back_a = lax.optimization_barrier((got_b, back_a))
    swap_b = swapped(got_b_again)
    [back_a] = pulled(job_a, [bf16], scale, shift, 0, back_a)
    [back_b] = pulled(
        [([swap_b], [second, other_first, got_a, got_b], [], False)], [bf16], scale, shift
    )
    home_a = sent(back_a, lambda g, x, c: (g, x + 1, 0) if c == 0 else (g - 1, x, 1))
    home_b = sent(back_b, lambda g, x, c: (g, x + 1, 1) if c == 0 else (g - 1, x, 0))
    first_total, second_total = pulled(
        [
            ([first], [second, other_first, got_a, got_b], [], True),
            ([second], [first, other_second, swap_a, swap_b], [], True),
        ],
        [f32, f32],
        both,
        None,
    )
    outputs = placed(first_total, home_a, None, 1)
    return tuple(placed(second_total, home_b, outputs, 0))


def by_arrays(images, texts, scale, shift):
    chips = lax.axis_size("in") // CORES
    f32, bf16 = jnp.float32, jnp.bfloat16
    back_texts = moved(texts, "grp", lambda i: i + 1)
    near_images = [moved(images, "in", lambda i, k=k: i - CORES * k) for k in range(1, chips)]
    images, texts = held([images, texts], scale, shift)
    core_images, core_texts = swapped(images), swapped(texts)
    far_images = [swapped(block) for block in near_images]
    far_texts = swapped(back_texts)
    own_texts = [texts, core_texts]
    group_images = [images, core_images] + near_images + far_images

    starts = pulled(
        [(near_images, own_texts, [], False)], [f32] * (chips - 1), scale, shift
    )
    [sent_texts] = pulled([([back_texts], group_images, [], False)], [bf16], scale, shift)
    sent_images = pulled(
        [(near_images, [back_texts, far_texts], starts, False)],
        [bf16] * (chips - 1),
        scale,
        shift,
    )
    sent_texts, *sent_images = lax.optimization_barrier((sent_texts, *sent_images))
    sent_images = [
        moved(block, "in", lambda i, k=k: i + CORES * k) for k, block in enumerate(sent_images, 1)
    ]
    sent_texts = moved(sent_texts, "grp", lambda i: i - 1)
    image_total, text_total = pulled(
        [
            ([images], own_texts + [back_texts, far_texts], [], True),
            ([texts], group_images, [], True),
        ],
        [f32, f32],
        scale,
        shift,
    )
    return tuple(summed([[image_total] + sent_images, [text_total, sent_texts]]))


def shards(images, texts, scale, shift):
    if lax.axis_size("in") == 2 * CORES:
        return by_roles(images, texts, scale, shift)
    return by_arrays(images, texts, scale, shift)


def solution(mesh):
    rows = P(("grp", "in"), None)
    return jax.shard_map(
        shards,
        mesh=mesh,
        in_specs=(rows, rows, P(), P()),
        out_specs=(rows, rows),
        check_vma=False,
    )
```

```python
import jax
import jax.numpy as jnp
from jax import lax
from jax.experimental import pallas as pl
from jax.experimental.pallas import tpu as pltpu
from jax.sharding import PartitionSpec as P

CORES = 2
VMEM = pl.BlockSpec(memory_space=pltpu.VMEM)
SMEM = pl.BlockSpec(memory_space=pltpu.SMEM)


def moved(array, axis, target):
    peers = lax.axis_size(axis)
    return lax.ppermute(array, axis, [(i, target(i) % peers) for i in range(peers)])


def swapped(array):
    return moved(array, "in", lambda i: i ^ 1)


def held(arrays, scale, shift):
    def kernel(scale_ref, shift_ref, *refs):
        sources, targets, sems = refs[: len(arrays)], refs[len(arrays) : -1], refs[-1]
        copies = [
            pltpu.make_async_copy(source, target, sems.at[i])
            for i, (source, target) in enumerate(zip(sources, targets))
        ]
        for copy in copies:
            copy.start()
        for copy in copies:
            copy.wait()

    return pl.pallas_call(
        kernel,
        out_shape=[jax.ShapeDtypeStruct(a.shape, a.dtype) for a in arrays],
        in_specs=[SMEM] * 2 + [pl.BlockSpec(memory_space=pl.ANY)] * len(arrays),
        out_specs=[VMEM] * len(arrays),
        scratch_shapes=[pltpu.SemaphoreType.DMA((len(arrays),))],
        compiler_params=pltpu.CompilerParams(vmem_limit_bytes=4 << 20),
    )(scale, shift, *arrays)


def pulled(jobs, out_types, scale, shift, only=None, into=None):
    height, width = jobs[0][0][0].shape
    kept = [] if into is None else [into]
    arrays = [a for rows, others, starts, _ in jobs for a in (*rows, *others, *starts)]

    scalars = [scale] if shift is None else [scale, shift]

    def kernel(*refs):
        scalar_refs, refs = refs[: len(scalars)], refs[len(scalars) :]

        def run():
            if shift is None:
                values = scalar_refs[0][0:1, 0:1], scalar_refs[0][1:2, 0:1]
            else:
                values = scalar_refs[0][0], scalar_refs[1][0]
            write(*values, refs[: len(arrays)], refs[len(arrays) + len(kept) :])

        if only is None:
            run()
        else:
            here = lax.rem(lax.axis_index("in"), CORES) == only
            pl.when(here)(run)

        if kept:

            @pl.when(jnp.logical_not(here))
            def _():
                refs[-1][...] = refs[-2][...]

    def write(scale_now, shift_now, in_refs, out_refs):
        in_refs, out_refs = iter(in_refs), iter(out_refs)
        for rows, others, starts, paired in jobs:
            row_refs = [next(in_refs) for _ in rows]
            other_refs = [next(in_refs) for _ in others]
            start_refs = [next(in_refs) for _ in starts]
            left = jnp.concatenate([ref[...] for ref in row_refs], axis=0)
            right = jnp.concatenate([ref[...] for ref in other_refs], axis=0)
            logits = lax.dot_general(
                left, right, (((1,), (1,)), ((), ())), preferred_element_type=jnp.float32
            )
            slope = jax.nn.sigmoid(scale_now * logits + shift_now)
            if paired:
                row_ids = lax.broadcasted_iota(jnp.int32, slope.shape, 0)
                col_ids = lax.broadcasted_iota(jnp.int32, slope.shape, 1)
                matched = (col_ids == row_ids) & (row_ids < height)
                slope = slope - matched.astype(jnp.float32)
            weights = (scale_now * slope).astype(jnp.bfloat16)
            terms = jnp.dot(weights, right, preferred_element_type=jnp.float32)
            for i in range(len(rows)):
                term = terms[i * height : (i + 1) * height]
                if starts:
                    term = term + start_refs[i][...]
                out_ref = next(out_refs)
                out_ref[...] = term.astype(out_ref.dtype)

    pairs = sum(height * height * len(rows) * len(others) for rows, others, _, _ in jobs)
    size = sum(a.size * a.dtype.itemsize for a in arrays)
    size += sum(height * width * jnp.dtype(t).itemsize for t in out_types)
    return pl.pallas_call(
        kernel,
        out_shape=[jax.ShapeDtypeStruct((height, width), t) for t in out_types],
        in_specs=[VMEM if shift is None else SMEM] * len(scalars)
        + [VMEM] * (len(arrays) + len(kept)),
        out_specs=[VMEM] * len(out_types),
        cost_estimate=pl.CostEstimate(
            flops=4 * pairs * width, bytes_accessed=size, transcendentals=pairs
        ),
        compiler_params=pltpu.CompilerParams(vmem_limit_bytes=2 * size + 16 * pairs + (4 << 20)),
    )(*scalars, *arrays, *kept)


def summed(sums):
    shape = sums[0][0].shape
    arrays = [a for blocks in sums for a in blocks]

    def kernel(*refs):
        in_refs, out_refs = iter(refs[: len(arrays)]), refs[len(arrays) :]
        for blocks, out_ref in zip(sums, out_refs):
            total = next(in_refs)[...]
            for _ in blocks[1:]:
                total = total + next(in_refs)[...].astype(jnp.float32)
            out_ref[...] = total.astype(out_ref.dtype)

    size = sum(a.size * a.dtype.itemsize for a in arrays)
    return pl.pallas_call(
        kernel,
        out_shape=[jax.ShapeDtypeStruct(shape, jnp.bfloat16) for _ in sums],
        in_specs=[VMEM] * len(arrays),
        out_specs=[VMEM] * len(sums),
        cost_estimate=pl.CostEstimate(flops=size, bytes_accessed=size, transcendentals=0),
        compiler_params=pltpu.CompilerParams(vmem_limit_bytes=2 * size + (4 << 20)),
    )(*arrays)


def placed(total, extra, kept, texts_on):
    shape, dtype = total.shape, jnp.bfloat16
    pieces = 2
    rows = shape[0] // pieces

    def kernel(total_ref, extra_ref, *refs):
        image_ref, text_ref, rounded_ref, sems = refs[-4:]
        is_text = lax.rem(lax.axis_index("in"), CORES) == texts_on

        def copy(piece, target_ref):
            part = pl.ds(piece * rows, rows)
            return pltpu.make_async_copy(rounded_ref.at[part], target_ref.at[part], sems.at[piece])

        for piece in range(pieces):
            part = pl.ds(piece * rows, rows)
            block = total_ref[part, :] + extra_ref[part, :].astype(jnp.float32)
            rounded_ref[part, :] = block.astype(dtype)
            pl.when(is_text)(lambda piece=piece: copy(piece, text_ref).start())
            pl.when(jnp.logical_not(is_text))(lambda piece=piece: copy(piece, image_ref).start())
        for piece in range(pieces):
            copy(piece, image_ref).wait()

    hbm = pl.BlockSpec(memory_space=pl.ANY)
    kept = [] if kept is None else list(kept)
    size = total.size * 4
    return pl.pallas_call(
        kernel,
        out_shape=[jax.ShapeDtypeStruct(shape, dtype)] * 2,
        in_specs=[VMEM] * 2 + [hbm] * len(kept),
        out_specs=[hbm] * 2,
        scratch_shapes=[pltpu.VMEM(shape, dtype), pltpu.SemaphoreType.DMA((pieces,))],
        input_output_aliases={2 + i: i for i in range(len(kept))},
        cost_estimate=pl.CostEstimate(flops=size, bytes_accessed=size, transcendentals=0),
        compiler_params=pltpu.CompilerParams(vmem_limit_bytes=4 * size + (4 << 20)),
    )(total, extra, *kept)


def opened():
    def kernel(out_ref):
        out_ref[...] = jnp.zeros_like(out_ref)

    return pl.pallas_call(
        kernel,
        out_shape=jax.ShapeDtypeStruct((8, 128), jnp.float32),
        out_specs=VMEM,
        cost_estimate=pl.CostEstimate(flops=10**10, bytes_accessed=2**26, transcendentals=0),
        compiler_params=pltpu.CompilerParams(vmem_limit_bytes=1 << 20),
    )()


def ranked(images, texts, opening):
    def kernel(image_ref, text_ref, opening_ref, first_ref, second_ref):
        core = lax.rem(lax.axis_index("in"), CORES)
        for number, sources in enumerate([(image_ref, text_ref), (text_ref, image_ref)]):

            @pl.when(core == number)
            def _(sources=sources):
                first_ref[...] = sources[0][...]
                second_ref[...] = sources[1][...]

    return pl.pallas_call(
        kernel,
        out_shape=[jax.ShapeDtypeStruct(images.shape, images.dtype)] * 2,
        in_specs=[VMEM] * 3,
        out_specs=[VMEM] * 2,
        compiler_params=pltpu.CompilerParams(vmem_limit_bytes=4 << 20),
    )(images, texts, opening)


def packed(scale, shift):
    def kernel(scale_ref, shift_ref, out_ref):
        out_ref[0:1, :] = jnp.full((1, 128), scale_ref[0], jnp.float32)
        out_ref[1:2, :] = jnp.full((1, 128), shift_ref[0], jnp.float32)

    return pl.pallas_call(
        kernel,
        out_shape=jax.ShapeDtypeStruct((2, 128), jnp.float32),
        in_specs=[SMEM] * 2,
        out_specs=VMEM,
        compiler_params=pltpu.CompilerParams(vmem_limit_bytes=1 << 20),
    )(scale, shift)


def by_roles(images, texts, scale, shift):
    groups, members = lax.axis_size("grp"), lax.axis_size("in")
    f32, bf16 = jnp.float32, jnp.bfloat16

    def sent(array, target):
        pairs = []
        for group in range(groups):
            for chip in range(members // CORES):
                for core in range(CORES):
                    to_group, to_chip, to_core = target(group, chip, core)
                    pairs.append(
                        (
                            group * members + chip * CORES + core,
                            to_group % groups * members + (to_chip % 2) * CORES + to_core,
                        )
                    )
        return lax.ppermute(array, ("grp", "in"), pairs)

    is_image_core = lax.rem(lax.axis_index("in"), CORES) == 0
    other_images, other_texts = swapped(images), swapped(texts)
    first, second = ranked(images, texts, opened())
    other_first = jnp.where(is_image_core, other_texts, other_images)
    other_second = jnp.where(is_image_core, other_images, other_texts)
    got_a, got_b = [
        sent(block, lambda g, x, c: (g, x + 1, 1) if c == 0 else (g + 1, x, 0))
        for block in (first, other_second)
    ]
    starts = pulled(
        [
            ([first], [second, other_first], [], True),
            ([second], [first, other_second], [], True),
        ],
        [f32, f32],
        scale,
        shift,
    )
    got_a, both = lax.optimization_barrier((got_a, packed(scale, shift)))
    swap_a = swapped(got_a)
    got_b, *starts = lax.optimization_barrier((got_b, *starts))
    half = swap_a.shape[0] // 2
    jobs_a = [
        ([rows], [second, other_first, got_a, got_b], [], False)
        for rows in (swap_a[:half], swap_a[half:])
    ]
    backs_a = pulled(jobs_a, [bf16] * 2, scale, shift, 1)
    got_b_again, *backs_a = lax.optimization_barrier((got_b, *backs_a))
    swap_b = swapped(got_b_again)
    backs_a = [
        pulled([job], [bf16], scale, shift, 0, back)[0] for job, back in zip(jobs_a, backs_a)
    ]
    [back_b] = pulled(
        [([swap_b], [second, other_first, got_a, got_b], [], False)], [bf16], scale, shift
    )
    home_a = jnp.concatenate(
        [
            sent(back, lambda g, x, c: (g, x + 1, 0) if c == 0 else (g - 1, x, 1))
            for back in backs_a
        ],
        axis=0,
    )
    home_b = sent(back_b, lambda g, x, c: (g, x + 1, 1) if c == 0 else (g - 1, x, 0))
    first_total, second_total = pulled(
        [
            ([first], [got_a, got_b], starts[:1], False),
            ([second], [swap_a, swap_b], starts[1:], False),
        ],
        [f32, f32],
        both,
        None,
    )
    outputs = placed(first_total, home_a, None, 1)
    return tuple(placed(second_total, home_b, outputs, 0))


def by_arrays(images, texts, scale, shift):
    chips = lax.axis_size("in") // CORES
    f32, bf16 = jnp.float32, jnp.bfloat16
    back_texts = moved(texts, "grp", lambda i: i + 1)
    near_images = [moved(images, "in", lambda i, k=k: i - CORES * k) for k in range(1, chips)]
    images, texts = held([images, texts], scale, shift)
    core_images, core_texts = swapped(images), swapped(texts)
    far_images = [swapped(block) for block in near_images]
    far_texts = swapped(back_texts)
    own_texts = [texts, core_texts]
    group_images = [images, core_images] + near_images + far_images

    starts = pulled(
        [(near_images, own_texts, [], False)], [f32] * (chips - 1), scale, shift
    )
    [sent_texts] = pulled([([back_texts], group_images, [], False)], [bf16], scale, shift)
    sent_images = pulled(
        [(near_images, [back_texts, far_texts], starts, False)],
        [bf16] * (chips - 1),
        scale,
        shift,
    )
    sent_texts, *sent_images = lax.optimization_barrier((sent_texts, *sent_images))
    sent_images = [
        moved(block, "in", lambda i, k=k: i + CORES * k) for k, block in enumerate(sent_images, 1)
    ]
    sent_texts = moved(sent_texts, "grp", lambda i: i - 1)
    image_total, text_total = pulled(
        [
            ([images], own_texts + [back_texts, far_texts], [], True),
            ([texts], group_images, [], True),
        ],
        [f32, f32],
        scale,
        shift,
    )
    return tuple(summed([[image_total] + sent_images, [text_total, sent_texts]]))


def shards(images, texts, scale, shift):
    if lax.axis_size("in") == 2 * CORES:
        return by_roles(images, texts, scale, shift)
    return by_arrays(images, texts, scale, shift)


def solution(mesh):
    rows = P(("grp", "in"), None)
    return jax.shard_map(
        shards,
        mesh=mesh,
        in_specs=(rows, rows, P(), P()),
        out_specs=(rows, rows),
        check_vma=False,
    )
```

```python
import jax
import jax.numpy as jnp
from jax import lax
from jax.experimental import pallas as pl
from jax.experimental.pallas import tpu as pltpu
from jax.sharding import PartitionSpec as P

CORES = 2
VMEM = pl.BlockSpec(memory_space=pltpu.VMEM)
SMEM = pl.BlockSpec(memory_space=pltpu.SMEM)


def moved(array, axis, target):
    peers = lax.axis_size(axis)
    return lax.ppermute(array, axis, [(i, target(i) % peers) for i in range(peers)])


def swapped(array):
    return moved(array, "in", lambda i: i ^ 1)


def held(arrays, scale, shift):
    def kernel(scale_ref, shift_ref, *refs):
        sources, targets, sems = refs[: len(arrays)], refs[len(arrays) : -1], refs[-1]
        copies = [
            pltpu.make_async_copy(source, target, sems.at[i])
            for i, (source, target) in enumerate(zip(sources, targets))
        ]
        for copy in copies:
            copy.start()
        for copy in copies:
            copy.wait()

    return pl.pallas_call(
        kernel,
        out_shape=[jax.ShapeDtypeStruct(a.shape, a.dtype) for a in arrays],
        in_specs=[SMEM] * 2 + [pl.BlockSpec(memory_space=pl.ANY)] * len(arrays),
        out_specs=[VMEM] * len(arrays),
        scratch_shapes=[pltpu.SemaphoreType.DMA((len(arrays),))],
        compiler_params=pltpu.CompilerParams(vmem_limit_bytes=4 << 20),
    )(scale, shift, *arrays)


def pulled(jobs, out_types, scale, shift, only=None, into=None):
    height, width = jobs[0][0][0].shape
    kept = [] if into is None else [into]
    arrays = [a for rows, others, starts, _ in jobs for a in (*rows, *others, *starts)]

    scalars = [scale] if shift is None else [scale, shift]

    def kernel(*refs):
        scalar_refs, refs = refs[: len(scalars)], refs[len(scalars) :]

        def run():
            if shift is None:
                values = scalar_refs[0][0:1, 0:1], scalar_refs[0][1:2, 0:1]
            else:
                values = scalar_refs[0][0], scalar_refs[1][0]
            write(*values, refs[: len(arrays)], refs[len(arrays) + len(kept) :])

        if only is None:
            run()
        else:
            here = lax.rem(lax.axis_index("in"), CORES) == only
            pl.when(here)(run)

        if kept:

            @pl.when(jnp.logical_not(here))
            def _():
                refs[-1][...] = refs[-2][...]

    def write(scale_now, shift_now, in_refs, out_refs):
        in_refs, out_refs = iter(in_refs), iter(out_refs)
        for rows, others, starts, paired in jobs:
            row_refs = [next(in_refs) for _ in rows]
            other_refs = [next(in_refs) for _ in others]
            start_refs = [next(in_refs) for _ in starts]
            left = jnp.concatenate([ref[...] for ref in row_refs], axis=0)
            right = jnp.concatenate([ref[...] for ref in other_refs], axis=0)
            logits = lax.dot_general(
                left, right, (((1,), (1,)), ((), ())), preferred_element_type=jnp.float32
            )
            slope = jax.nn.sigmoid(scale_now * logits + shift_now)
            if paired:
                row_ids = lax.broadcasted_iota(jnp.int32, slope.shape, 0)
                col_ids = lax.broadcasted_iota(jnp.int32, slope.shape, 1)
                matched = (col_ids == row_ids) & (row_ids < height)
                slope = slope - matched.astype(jnp.float32)
            weights = (scale_now * slope).astype(jnp.bfloat16)
            terms = jnp.dot(weights, right, preferred_element_type=jnp.float32)
            for i in range(len(rows)):
                term = terms[i * height : (i + 1) * height]
                if starts:
                    term = term + start_refs[i][...]
                out_ref = next(out_refs)
                out_ref[...] = term.astype(out_ref.dtype)

    pairs = sum(height * height * len(rows) * len(others) for rows, others, _, _ in jobs)
    size = sum(a.size * a.dtype.itemsize for a in arrays)
    size += sum(height * width * jnp.dtype(t).itemsize for t in out_types)
    return pl.pallas_call(
        kernel,
        out_shape=[jax.ShapeDtypeStruct((height, width), t) for t in out_types],
        in_specs=[VMEM if shift is None else SMEM] * len(scalars)
        + [VMEM] * (len(arrays) + len(kept)),
        out_specs=[VMEM] * len(out_types),
        cost_estimate=pl.CostEstimate(
            flops=4 * pairs * width, bytes_accessed=size, transcendentals=pairs
        ),
        compiler_params=pltpu.CompilerParams(vmem_limit_bytes=2 * size + 16 * pairs + (4 << 20)),
    )(*scalars, *arrays, *kept)


def summed(sums):
    shape = sums[0][0].shape
    arrays = [a for blocks in sums for a in blocks]

    def kernel(*refs):
        in_refs, out_refs = iter(refs[: len(arrays)]), refs[len(arrays) :]
        for blocks, out_ref in zip(sums, out_refs):
            total = next(in_refs)[...]
            for _ in blocks[1:]:
                total = total + next(in_refs)[...].astype(jnp.float32)
            out_ref[...] = total.astype(out_ref.dtype)

    size = sum(a.size * a.dtype.itemsize for a in arrays)
    return pl.pallas_call(
        kernel,
        out_shape=[jax.ShapeDtypeStruct(shape, jnp.bfloat16) for _ in sums],
        in_specs=[VMEM] * len(arrays),
        out_specs=[VMEM] * len(sums),
        cost_estimate=pl.CostEstimate(flops=size, bytes_accessed=size, transcendentals=0),
        compiler_params=pltpu.CompilerParams(vmem_limit_bytes=2 * size + (4 << 20)),
    )(*arrays)


def placed(total, extra, kept, texts_on):
    shape, dtype = total.shape, jnp.bfloat16
    pieces = 4
    rows = shape[0] // pieces

    def kernel(total_ref, extra_ref, *refs):
        image_ref, text_ref, rounded_ref, sems = refs[-4:]
        is_text = lax.rem(lax.axis_index("in"), CORES) == texts_on

        def copy(piece, target_ref):
            part = pl.ds(piece * rows, rows)
            return pltpu.make_async_copy(rounded_ref.at[part], target_ref.at[part], sems.at[piece])

        for piece in range(pieces):
            part = pl.ds(piece * rows, rows)
            block = total_ref[part, :] + extra_ref[part, :].astype(jnp.float32)
            rounded_ref[part, :] = block.astype(dtype)
            pl.when(is_text)(lambda piece=piece: copy(piece, text_ref).start())
            pl.when(jnp.logical_not(is_text))(lambda piece=piece: copy(piece, image_ref).start())
        for piece in range(pieces):
            copy(piece, image_ref).wait()

    hbm = pl.BlockSpec(memory_space=pl.ANY)
    kept = [] if kept is None else list(kept)
    size = total.size * 4
    return pl.pallas_call(
        kernel,
        out_shape=[jax.ShapeDtypeStruct(shape, dtype)] * 2,
        in_specs=[VMEM] * 2 + [hbm] * len(kept),
        out_specs=[hbm] * 2,
        scratch_shapes=[pltpu.VMEM(shape, dtype), pltpu.SemaphoreType.DMA((pieces,))],
        input_output_aliases={2 + i: i for i in range(len(kept))},
        cost_estimate=pl.CostEstimate(flops=size, bytes_accessed=size, transcendentals=0),
        compiler_params=pltpu.CompilerParams(vmem_limit_bytes=4 * size + (4 << 20)),
    )(total, extra, *kept)


def opened():
    def kernel(out_ref):
        out_ref[...] = jnp.zeros_like(out_ref)

    return pl.pallas_call(
        kernel,
        out_shape=jax.ShapeDtypeStruct((8, 128), jnp.float32),
        out_specs=VMEM,
        cost_estimate=pl.CostEstimate(flops=10**10, bytes_accessed=2**26, transcendentals=0),
        compiler_params=pltpu.CompilerParams(vmem_limit_bytes=1 << 20),
    )()


def ranked(images, texts, opening):
    def kernel(image_ref, text_ref, opening_ref, first_ref, second_ref):
        core = lax.rem(lax.axis_index("in"), CORES)
        for number, sources in enumerate([(image_ref, text_ref), (text_ref, image_ref)]):

            @pl.when(core == number)
            def _(sources=sources):
                first_ref[...] = sources[0][...]
                second_ref[...] = sources[1][...]

    return pl.pallas_call(
        kernel,
        out_shape=[jax.ShapeDtypeStruct(images.shape, images.dtype)] * 2,
        in_specs=[VMEM] * 3,
        out_specs=[VMEM] * 2,
        compiler_params=pltpu.CompilerParams(vmem_limit_bytes=4 << 20),
    )(images, texts, opening)


def packed(scale, shift):
    def kernel(scale_ref, shift_ref, out_ref):
        out_ref[0:1, :] = jnp.full((1, 128), scale_ref[0], jnp.float32)
        out_ref[1:2, :] = jnp.full((1, 128), shift_ref[0], jnp.float32)

    return pl.pallas_call(
        kernel,
        out_shape=jax.ShapeDtypeStruct((2, 128), jnp.float32),
        in_specs=[SMEM] * 2,
        out_specs=VMEM,
        compiler_params=pltpu.CompilerParams(vmem_limit_bytes=1 << 20),
    )(scale, shift)


def by_roles(images, texts, scale, shift):
    groups, members = lax.axis_size("grp"), lax.axis_size("in")
    f32, bf16 = jnp.float32, jnp.bfloat16

    def sent(array, target):
        pairs = []
        for group in range(groups):
            for chip in range(members // CORES):
                for core in range(CORES):
                    to_group, to_chip, to_core = target(group, chip, core)
                    pairs.append(
                        (
                            group * members + chip * CORES + core,
                            to_group % groups * members + (to_chip % 2) * CORES + to_core,
                        )
                    )
        return lax.ppermute(array, ("grp", "in"), pairs)

    is_image_core = lax.rem(lax.axis_index("in"), CORES) == 0
    other_images, other_texts = swapped(images), swapped(texts)
    first, second = ranked(images, texts, opened())
    other_first = jnp.where(is_image_core, other_texts, other_images)
    other_second = jnp.where(is_image_core, other_images, other_texts)
    got_a, got_b = [
        sent(block, lambda g, x, c: (g, x + 1, 1) if c == 0 else (g + 1, x, 0))
        for block in (first, other_second)
    ]
    starts = pulled(
        [
            ([first], [second, other_first], [], True),
            ([second], [first, other_second], [], True),
        ],
        [f32, f32],
        scale,
        shift,
    )
    got_a, both = lax.optimization_barrier((got_a, packed(scale, shift)))
    swap_a = swapped(got_a)
    got_b, *starts = lax.optimization_barrier((got_b, *starts))
    job_a = [([swap_a], [second, other_first, got_a, got_b], [], False)]
    [back_a] = pulled(job_a, [bf16], scale, shift, 1)
    got_b_again, back_a = lax.optimization_barrier((got_b, back_a))
    swap_b = swapped(got_b_again)
    [back_a] = pulled(job_a, [bf16], scale, shift, 0, back_a)
    [back_b] = pulled(
        [([swap_b], [second, other_first, got_a, got_b], [], False)], [bf16], scale, shift
    )
    home_a = sent(back_a, lambda g, x, c: (g, x + 1, 0) if c == 0 else (g - 1, x, 1))
    home_b = sent(back_b, lambda g, x, c: (g, x + 1, 1) if c == 0 else (g - 1, x, 0))
    first_total, second_total = pulled(
        [
            ([first], [got_a, got_b], starts[:1], False),
            ([second], [swap_a, swap_b], starts[1:], False),
        ],
        [f32, f32],
        both,
        None,
    )
    outputs = placed(first_total, home_a, None, 1)
    return tuple(placed(second_total, home_b, outputs, 0))


def by_arrays(images, texts, scale, shift):
    chips = lax.axis_size("in") // CORES
    f32, bf16 = jnp.float32, jnp.bfloat16
    back_texts = moved(texts, "grp", lambda i: i + 1)
    near_images = [moved(images, "in", lambda i, k=k: i - CORES * k) for k in range(1, chips)]
    images, texts = held([images, texts], scale, shift)
    core_images, core_texts = swapped(images), swapped(texts)
    far_images = [swapped(block) for block in near_images]
    far_texts = swapped(back_texts)
    own_texts = [texts, core_texts]
    group_images = [images, core_images] + near_images + far_images

    starts = pulled(
        [(near_images, own_texts, [], False)], [f32] * (chips - 1), scale, shift
    )
    [sent_texts] = pulled([([back_texts], group_images, [], False)], [bf16], scale, shift)
    sent_images = pulled(
        [(near_images, [back_texts, far_texts], starts, False)],
        [bf16] * (chips - 1),
        scale,
        shift,
    )
    sent_texts, *sent_images = lax.optimization_barrier((sent_texts, *sent_images))
    sent_images = [
        moved(block, "in", lambda i, k=k: i + CORES * k) for k, block in enumerate(sent_images, 1)
    ]
    sent_texts = moved(sent_texts, "grp", lambda i: i - 1)
    image_total, text_total = pulled(
        [
            ([images], own_texts + [back_texts, far_texts], [], True),
            ([texts], group_images, [], True),
        ],
        [f32, f32],
        scale,
        shift,
    )
    return tuple(summed([[image_total] + sent_images, [text_total, sent_texts]]))


def shards(images, texts, scale, shift):
    if lax.axis_size("in") == 2 * CORES:
        return by_roles(images, texts, scale, shift)
    return by_arrays(images, texts, scale, shift)


def solution(mesh):
    rows = P(("grp", "in"), None)
    return jax.shard_map(
        shards,
        mesh=mesh,
        in_specs=(rows, rows, P(), P()),
        out_specs=(rows, rows),
        check_vma=False,
    )
```

```python
import jax
import jax.numpy as jnp
from jax import lax
from jax.experimental import pallas as pl
from jax.experimental.pallas import tpu as pltpu
from jax.sharding import PartitionSpec as P

CORES = 2
VMEM = pl.BlockSpec(memory_space=pltpu.VMEM)
SMEM = pl.BlockSpec(memory_space=pltpu.SMEM)


def moved(array, axis, target):
    peers = lax.axis_size(axis)
    return lax.ppermute(array, axis, [(i, target(i) % peers) for i in range(peers)])


def swapped(array):
    return moved(array, "in", lambda i: i ^ 1)


def held(arrays, scale, shift):
    def kernel(scale_ref, shift_ref, *refs):
        sources, targets, sems = refs[: len(arrays)], refs[len(arrays) : -1], refs[-1]
        copies = [
            pltpu.make_async_copy(source, target, sems.at[i])
            for i, (source, target) in enumerate(zip(sources, targets))
        ]
        for copy in copies:
            copy.start()
        for copy in copies:
            copy.wait()

    return pl.pallas_call(
        kernel,
        out_shape=[jax.ShapeDtypeStruct(a.shape, a.dtype) for a in arrays],
        in_specs=[SMEM] * 2 + [pl.BlockSpec(memory_space=pl.ANY)] * len(arrays),
        out_specs=[VMEM] * len(arrays),
        scratch_shapes=[pltpu.SemaphoreType.DMA((len(arrays),))],
        compiler_params=pltpu.CompilerParams(vmem_limit_bytes=4 << 20),
    )(scale, shift, *arrays)


def pulled(jobs, out_types, scale, shift, only=None, into=None):
    height, width = jobs[0][0][0].shape
    kept = [] if into is None else [into]
    arrays = [a for rows, others, starts, _ in jobs for a in (*rows, *others, *starts)]

    scalars = [scale] if shift is None else [scale, shift]

    def kernel(*refs):
        scalar_refs, refs = refs[: len(scalars)], refs[len(scalars) :]

        def run():
            if shift is None:
                values = scalar_refs[0][0:1, 0:1], scalar_refs[0][1:2, 0:1]
            else:
                values = scalar_refs[0][0], scalar_refs[1][0]
            write(*values, refs[: len(arrays)], refs[len(arrays) + len(kept) :])

        if only is None:
            run()
        else:
            here = lax.rem(lax.axis_index("in"), CORES) == only
            pl.when(here)(run)

        if kept:

            @pl.when(jnp.logical_not(here))
            def _():
                refs[-1][...] = refs[-2][...]

    def write(scale_now, shift_now, in_refs, out_refs):
        in_refs, out_refs = iter(in_refs), iter(out_refs)
        for rows, others, starts, paired in jobs:
            row_refs = [next(in_refs) for _ in rows]
            other_refs = [next(in_refs) for _ in others]
            start_refs = [next(in_refs) for _ in starts]
            left = jnp.concatenate([ref[...] for ref in row_refs], axis=0)
            right = jnp.concatenate([ref[...] for ref in other_refs], axis=0)
            logits = lax.dot_general(
                left, right, (((1,), (1,)), ((), ())), preferred_element_type=jnp.float32
            )
            slope = jax.nn.sigmoid(scale_now * logits + shift_now)
            if paired:
                row_ids = lax.broadcasted_iota(jnp.int32, slope.shape, 0)
                col_ids = lax.broadcasted_iota(jnp.int32, slope.shape, 1)
                matched = (col_ids == row_ids) & (row_ids < height)
                slope = slope - matched.astype(jnp.float32)
            weights = (scale_now * slope).astype(jnp.bfloat16)
            terms = jnp.dot(weights, right, preferred_element_type=jnp.float32)
            for i in range(len(rows)):
                term = terms[i * height : (i + 1) * height]
                if starts:
                    term = term + start_refs[i][...]
                out_ref = next(out_refs)
                out_ref[...] = term.astype(out_ref.dtype)

    pairs = sum(height * height * len(rows) * len(others) for rows, others, _, _ in jobs)
    size = sum(a.size * a.dtype.itemsize for a in arrays)
    size += sum(height * width * jnp.dtype(t).itemsize for t in out_types)
    return pl.pallas_call(
        kernel,
        out_shape=[jax.ShapeDtypeStruct((height, width), t) for t in out_types],
        in_specs=[VMEM if shift is None else SMEM] * len(scalars)
        + [VMEM] * (len(arrays) + len(kept)),
        out_specs=[VMEM] * len(out_types),
        cost_estimate=pl.CostEstimate(
            flops=4 * pairs * width, bytes_accessed=size, transcendentals=pairs
        ),
        compiler_params=pltpu.CompilerParams(vmem_limit_bytes=2 * size + 16 * pairs + (4 << 20)),
    )(*scalars, *arrays, *kept)


def summed(sums):
    shape = sums[0][0].shape
    arrays = [a for blocks in sums for a in blocks]

    def kernel(*refs):
        in_refs, out_refs = iter(refs[: len(arrays)]), refs[len(arrays) :]
        for blocks, out_ref in zip(sums, out_refs):
            total = next(in_refs)[...]
            for _ in blocks[1:]:
                total = total + next(in_refs)[...].astype(jnp.float32)
            out_ref[...] = total.astype(out_ref.dtype)

    size = sum(a.size * a.dtype.itemsize for a in arrays)
    return pl.pallas_call(
        kernel,
        out_shape=[jax.ShapeDtypeStruct(shape, jnp.bfloat16) for _ in sums],
        in_specs=[VMEM] * len(arrays),
        out_specs=[VMEM] * len(sums),
        cost_estimate=pl.CostEstimate(flops=size, bytes_accessed=size, transcendentals=0),
        compiler_params=pltpu.CompilerParams(vmem_limit_bytes=2 * size + (4 << 20)),
    )(*arrays)


def placed(total, extra, kept, texts_on):
    shape, dtype = total.shape, jnp.bfloat16
    pieces = 1
    rows = shape[0] // pieces

    def kernel(total_ref, extra_ref, *refs):
        image_ref, text_ref, rounded_ref, sems = refs[-4:]
        is_text = lax.rem(lax.axis_index("in"), CORES) == texts_on

        def copy(piece, target_ref):
            part = pl.ds(piece * rows, rows)
            return pltpu.make_async_copy(rounded_ref.at[part], target_ref.at[part], sems.at[piece])

        for piece in range(pieces):
            part = pl.ds(piece * rows, rows)
            block = total_ref[part, :] + extra_ref[part, :].astype(jnp.float32)
            rounded_ref[part, :] = block.astype(dtype)
            pl.when(is_text)(lambda piece=piece: copy(piece, text_ref).start())
            pl.when(jnp.logical_not(is_text))(lambda piece=piece: copy(piece, image_ref).start())
        for piece in range(pieces):
            copy(piece, image_ref).wait()

    hbm = pl.BlockSpec(memory_space=pl.ANY)
    kept = [] if kept is None else list(kept)
    size = total.size * 4
    return pl.pallas_call(
        kernel,
        out_shape=[jax.ShapeDtypeStruct(shape, dtype)] * 2,
        in_specs=[VMEM] * 2 + [hbm] * len(kept),
        out_specs=[hbm] * 2,
        scratch_shapes=[pltpu.VMEM(shape, dtype), pltpu.SemaphoreType.DMA((pieces,))],
        input_output_aliases={2 + i: i for i in range(len(kept))},
        cost_estimate=pl.CostEstimate(flops=size, bytes_accessed=size, transcendentals=0),
        compiler_params=pltpu.CompilerParams(vmem_limit_bytes=4 * size + (4 << 20)),
    )(total, extra, *kept)


def opened():
    def kernel(out_ref):
        out_ref[...] = jnp.zeros_like(out_ref)

    return pl.pallas_call(
        kernel,
        out_shape=jax.ShapeDtypeStruct((8, 128), jnp.float32),
        out_specs=VMEM,
        cost_estimate=pl.CostEstimate(flops=10**10, bytes_accessed=2**26, transcendentals=0),
        compiler_params=pltpu.CompilerParams(vmem_limit_bytes=1 << 20),
    )()


def ranked(images, texts, opening):
    def kernel(image_ref, text_ref, opening_ref, first_ref, second_ref):
        core = lax.rem(lax.axis_index("in"), CORES)
        for number, sources in enumerate([(image_ref, text_ref), (text_ref, image_ref)]):

            @pl.when(core == number)
            def _(sources=sources):
                first_ref[...] = sources[0][...]
                second_ref[...] = sources[1][...]

    return pl.pallas_call(
        kernel,
        out_shape=[jax.ShapeDtypeStruct(images.shape, images.dtype)] * 2,
        in_specs=[VMEM] * 3,
        out_specs=[VMEM] * 2,
        compiler_params=pltpu.CompilerParams(vmem_limit_bytes=4 << 20),
    )(images, texts, opening)


def packed(scale, shift):
    def kernel(scale_ref, shift_ref, out_ref):
        out_ref[0:1, :] = jnp.full((1, 128), scale_ref[0], jnp.float32)
        out_ref[1:2, :] = jnp.full((1, 128), shift_ref[0], jnp.float32)

    return pl.pallas_call(
        kernel,
        out_shape=jax.ShapeDtypeStruct((2, 128), jnp.float32),
        in_specs=[SMEM] * 2,
        out_specs=VMEM,
        compiler_params=pltpu.CompilerParams(vmem_limit_bytes=1 << 20),
    )(scale, shift)


def by_roles(images, texts, scale, shift):
    groups, members = lax.axis_size("grp"), lax.axis_size("in")
    f32, bf16 = jnp.float32, jnp.bfloat16

    def sent(array, target):
        pairs = []
        for group in range(groups):
            for chip in range(members // CORES):
                for core in range(CORES):
                    to_group, to_chip, to_core = target(group, chip, core)
                    pairs.append(
                        (
                            group * members + chip * CORES + core,
                            to_group % groups * members + (to_chip % 2) * CORES + to_core,
                        )
                    )
        return lax.ppermute(array, ("grp", "in"), pairs)

    is_image_core = lax.rem(lax.axis_index("in"), CORES) == 0
    other_images, other_texts = swapped(images), swapped(texts)
    first, second = ranked(images, texts, opened())
    other_first = jnp.where(is_image_core, other_texts, other_images)
    other_second = jnp.where(is_image_core, other_images, other_texts)
    got_a, got_b = [
        sent(block, lambda g, x, c: (g, x + 1, 1) if c == 0 else (g + 1, x, 0))
        for block in (first, other_second)
    ]
    starts = pulled(
        [
            ([first], [second, other_first], [], True),
            ([second], [first, other_second], [], True),
        ],
        [f32, f32],
        scale,
        shift,
    )
    got_a, both = lax.optimization_barrier((got_a, packed(scale, shift)))
    swap_a = swapped(got_a)
    got_b, *starts = lax.optimization_barrier((got_b, *starts))
    job_a = [([swap_a], [second, other_first, got_a, got_b], [], False)]
    [back_a] = pulled(job_a, [bf16], scale, shift, 1)
    got_b_again, back_a = lax.optimization_barrier((got_b, back_a))
    swap_b = swapped(got_b_again)
    [back_a] = pulled(job_a, [bf16], scale, shift, 0, back_a)
    [back_b] = pulled(
        [([swap_b], [second, other_first, got_a, got_b], [], False)], [bf16], scale, shift
    )
    home_a = sent(back_a, lambda g, x, c: (g, x + 1, 0) if c == 0 else (g - 1, x, 1))
    home_b = sent(back_b, lambda g, x, c: (g, x + 1, 1) if c == 0 else (g - 1, x, 0))
    first_total, second_total = pulled(
        [
            ([first], [got_a, got_b], starts[:1], False),
            ([second], [swap_a, swap_b], starts[1:], False),
        ],
        [f32, f32],
        both,
        None,
    )
    outputs = placed(first_total, home_a, None, 1)
    return tuple(placed(second_total, home_b, outputs, 0))


def by_arrays(images, texts, scale, shift):
    chips = lax.axis_size("in") // CORES
    f32, bf16 = jnp.float32, jnp.bfloat16
    back_texts = moved(texts, "grp", lambda i: i + 1)
    near_images = [moved(images, "in", lambda i, k=k: i - CORES * k) for k in range(1, chips)]
    images, texts = held([images, texts], scale, shift)
    core_images, core_texts = swapped(images), swapped(texts)
    far_images = [swapped(block) for block in near_images]
    far_texts = swapped(back_texts)
    own_texts = [texts, core_texts]
    group_images = [images, core_images] + near_images + far_images

    starts = pulled(
        [(near_images, own_texts, [], False)], [f32] * (chips - 1), scale, shift
    )
    [sent_texts] = pulled([([back_texts], group_images, [], False)], [bf16], scale, shift)
    sent_images = pulled(
        [(near_images, [back_texts, far_texts], starts, False)],
        [bf16] * (chips - 1),
        scale,
        shift,
    )
    sent_texts, *sent_images = lax.optimization_barrier((sent_texts, *sent_images))
    sent_images = [
        moved(block, "in", lambda i, k=k: i + CORES * k) for k, block in enumerate(sent_images, 1)
    ]
    sent_texts = moved(sent_texts, "grp", lambda i: i - 1)
    image_total, text_total = pulled(
        [
            ([images], own_texts + [back_texts, far_texts], [], True),
            ([texts], group_images, [], True),
        ],
        [f32, f32],
        scale,
        shift,
    )
    return tuple(summed([[image_total] + sent_images, [text_total, sent_texts]]))


def shards(images, texts, scale, shift):
    if lax.axis_size("in") == 2 * CORES:
        return by_roles(images, texts, scale, shift)
    return by_arrays(images, texts, scale, shift)


def solution(mesh):
    rows = P(("grp", "in"), None)
    return jax.shard_map(
        shards,
        mesh=mesh,
        in_specs=(rows, rows, P(), P()),
        out_specs=(rows, rows),
        check_vma=False,
    )
```

```python
import jax
import jax.numpy as jnp
from jax import lax
from jax.experimental import pallas as pl
from jax.experimental.pallas import tpu as pltpu
from jax.sharding import PartitionSpec as P

CORES = 2
VMEM = pl.BlockSpec(memory_space=pltpu.VMEM)
SMEM = pl.BlockSpec(memory_space=pltpu.SMEM)


def moved(array, axis, target):
    peers = lax.axis_size(axis)
    return lax.ppermute(array, axis, [(i, target(i) % peers) for i in range(peers)])


def swapped(array):
    return moved(array, "in", lambda i: i ^ 1)


def held(arrays, scale, shift):
    def kernel(scale_ref, shift_ref, *refs):
        sources, targets, sems = refs[: len(arrays)], refs[len(arrays) : -1], refs[-1]
        copies = [
            pltpu.make_async_copy(source, target, sems.at[i])
            for i, (source, target) in enumerate(zip(sources, targets))
        ]
        for copy in copies:
            copy.start()
        for copy in copies:
            copy.wait()

    return pl.pallas_call(
        kernel,
        out_shape=[jax.ShapeDtypeStruct(a.shape, a.dtype) for a in arrays],
        in_specs=[SMEM] * 2 + [pl.BlockSpec(memory_space=pl.ANY)] * len(arrays),
        out_specs=[VMEM] * len(arrays),
        scratch_shapes=[pltpu.SemaphoreType.DMA((len(arrays),))],
        compiler_params=pltpu.CompilerParams(vmem_limit_bytes=4 << 20),
    )(scale, shift, *arrays)


def pulled(jobs, out_types, scale, shift, only=None, into=None):
    height, width = jobs[0][0][0].shape
    kept = [] if into is None else [into]
    arrays = [a for rows, others, starts, _ in jobs for a in (*rows, *others, *starts)]

    scalars = [scale] if shift is None else [scale, shift]

    def kernel(*refs):
        scalar_refs, refs = refs[: len(scalars)], refs[len(scalars) :]

        def run():
            if shift is None:
                values = scalar_refs[0][0:1, 0:1], scalar_refs[0][1:2, 0:1]
            else:
                values = scalar_refs[0][0], scalar_refs[1][0]
            write(*values, refs[: len(arrays)], refs[len(arrays) + len(kept) :])

        if only is None:
            run()
        else:
            here = lax.rem(lax.axis_index("in"), CORES) == only
            pl.when(here)(run)

        if kept:

            @pl.when(jnp.logical_not(here))
            def _():
                refs[-1][...] = refs[-2][...]

    def write(scale_now, shift_now, in_refs, out_refs):
        in_refs, out_refs = iter(in_refs), iter(out_refs)
        for rows, others, starts, paired in jobs:
            row_refs = [next(in_refs) for _ in rows]
            other_refs = [next(in_refs) for _ in others]
            start_refs = [next(in_refs) for _ in starts]
            left = jnp.concatenate([ref[...] for ref in row_refs], axis=0)
            right = jnp.concatenate([ref[...] for ref in other_refs], axis=0)
            logits = lax.dot_general(
                left, right, (((1,), (1,)), ((), ())), preferred_element_type=jnp.float32
            )
            slope = jax.nn.sigmoid(scale_now * logits + shift_now)
            if paired:
                row_ids = lax.broadcasted_iota(jnp.int32, slope.shape, 0)
                col_ids = lax.broadcasted_iota(jnp.int32, slope.shape, 1)
                matched = (col_ids == row_ids) & (row_ids < height)
                slope = slope - matched.astype(jnp.float32)
            weights = (scale_now * slope).astype(jnp.bfloat16)
            terms = jnp.dot(weights, right, preferred_element_type=jnp.float32)
            for i in range(len(rows)):
                term = terms[i * height : (i + 1) * height]
                if starts:
                    term = term + start_refs[i][...]
                out_ref = next(out_refs)
                out_ref[...] = term.astype(out_ref.dtype)

    pairs = sum(height * height * len(rows) * len(others) for rows, others, _, _ in jobs)
    size = sum(a.size * a.dtype.itemsize for a in arrays)
    size += sum(height * width * jnp.dtype(t).itemsize for t in out_types)
    return pl.pallas_call(
        kernel,
        out_shape=[jax.ShapeDtypeStruct((height, width), t) for t in out_types],
        in_specs=[VMEM if shift is None else SMEM] * len(scalars)
        + [VMEM] * (len(arrays) + len(kept)),
        out_specs=[VMEM] * len(out_types),
        cost_estimate=pl.CostEstimate(
            flops=4 * pairs * width, bytes_accessed=size, transcendentals=pairs
        ),
        compiler_params=pltpu.CompilerParams(vmem_limit_bytes=2 * size + 16 * pairs + (4 << 20)),
    )(*scalars, *arrays, *kept)


def summed(sums):
    shape = sums[0][0].shape
    arrays = [a for blocks in sums for a in blocks]

    def kernel(*refs):
        in_refs, out_refs = iter(refs[: len(arrays)]), refs[len(arrays) :]
        for blocks, out_ref in zip(sums, out_refs):
            total = next(in_refs)[...]
            for _ in blocks[1:]:
                total = total + next(in_refs)[...].astype(jnp.float32)
            out_ref[...] = total.astype(out_ref.dtype)

    size = sum(a.size * a.dtype.itemsize for a in arrays)
    return pl.pallas_call(
        kernel,
        out_shape=[jax.ShapeDtypeStruct(shape, jnp.bfloat16) for _ in sums],
        in_specs=[VMEM] * len(arrays),
        out_specs=[VMEM] * len(sums),
        cost_estimate=pl.CostEstimate(flops=size, bytes_accessed=size, transcendentals=0),
        compiler_params=pltpu.CompilerParams(vmem_limit_bytes=2 * size + (4 << 20)),
    )(*arrays)


def placed(total, extra, kept, texts_on):
    shape, dtype = total.shape, jnp.bfloat16
    pieces = 2
    rows = shape[0] // pieces

    def kernel(total_ref, extra_ref, *refs):
        image_ref, text_ref, rounded_ref, sems = refs[-4:]
        is_text = lax.rem(lax.axis_index("in"), CORES) == texts_on

        def copy(piece, target_ref):
            part = pl.ds(piece * rows, rows)
            return pltpu.make_async_copy(rounded_ref.at[part], target_ref.at[part], sems.at[piece])

        for piece in range(pieces):
            part = pl.ds(piece * rows, rows)
            block = total_ref[part, :] + extra_ref[part, :].astype(jnp.float32)
            rounded_ref[part, :] = block.astype(dtype)
            pl.when(is_text)(lambda piece=piece: copy(piece, text_ref).start())
            pl.when(jnp.logical_not(is_text))(lambda piece=piece: copy(piece, image_ref).start())
        for piece in range(pieces):
            copy(piece, image_ref).wait()

    hbm = pl.BlockSpec(memory_space=pl.ANY)
    kept = [] if kept is None else list(kept)
    size = total.size * 4
    return pl.pallas_call(
        kernel,
        out_shape=[jax.ShapeDtypeStruct(shape, dtype)] * 2,
        in_specs=[VMEM] * 2 + [hbm] * len(kept),
        out_specs=[hbm] * 2,
        scratch_shapes=[pltpu.VMEM(shape, dtype), pltpu.SemaphoreType.DMA((pieces,))],
        input_output_aliases={2 + i: i for i in range(len(kept))},
        cost_estimate=pl.CostEstimate(flops=size, bytes_accessed=size, transcendentals=0),
        compiler_params=pltpu.CompilerParams(vmem_limit_bytes=4 * size + (4 << 20)),
    )(total, extra, *kept)


def opened():
    def kernel(out_ref):
        out_ref[...] = jnp.zeros_like(out_ref)

    return pl.pallas_call(
        kernel,
        out_shape=jax.ShapeDtypeStruct((8, 128), jnp.float32),
        out_specs=VMEM,
        cost_estimate=pl.CostEstimate(flops=10**10, bytes_accessed=2**26, transcendentals=0),
        compiler_params=pltpu.CompilerParams(vmem_limit_bytes=1 << 20),
    )()


def ranked(images, texts, opening):
    def kernel(image_ref, text_ref, opening_ref, first_ref, second_ref):
        core = lax.rem(lax.axis_index("in"), CORES)
        for number, sources in enumerate([(image_ref, text_ref), (text_ref, image_ref)]):

            @pl.when(core == number)
            def _(sources=sources):
                first_ref[...] = sources[0][...]
                second_ref[...] = sources[1][...]

    return pl.pallas_call(
        kernel,
        out_shape=[jax.ShapeDtypeStruct(images.shape, images.dtype)] * 2,
        in_specs=[VMEM] * 3,
        out_specs=[VMEM] * 2,
        compiler_params=pltpu.CompilerParams(vmem_limit_bytes=4 << 20),
    )(images, texts, opening)


def packed(scale, shift):
    def kernel(scale_ref, shift_ref, out_ref):
        out_ref[0:1, :] = jnp.full((1, 128), scale_ref[0], jnp.float32)
        out_ref[1:2, :] = jnp.full((1, 128), shift_ref[0], jnp.float32)

    return pl.pallas_call(
        kernel,
        out_shape=jax.ShapeDtypeStruct((2, 128), jnp.float32),
        in_specs=[SMEM] * 2,
        out_specs=VMEM,
        compiler_params=pltpu.CompilerParams(vmem_limit_bytes=1 << 20),
    )(scale, shift)


def by_roles(images, texts, scale, shift):
    groups, members = lax.axis_size("grp"), lax.axis_size("in")
    f32, bf16 = jnp.float32, jnp.bfloat16

    def sent(array, target):
        pairs = []
        for group in range(groups):
            for chip in range(members // CORES):
                for core in range(CORES):
                    to_group, to_chip, to_core = target(group, chip, core)
                    pairs.append(
                        (
                            group * members + chip * CORES + core,
                            to_group % groups * members + (to_chip % 2) * CORES + to_core,
                        )
                    )
        return lax.ppermute(array, ("grp", "in"), pairs)

    is_image_core = lax.rem(lax.axis_index("in"), CORES) == 0
    other_images, other_texts = swapped(images), swapped(texts)
    first, second = ranked(images, texts, opened())
    other_first = jnp.where(is_image_core, other_texts, other_images)
    other_second = jnp.where(is_image_core, other_images, other_texts)
    got_a, got_b = [
        sent(block, lambda g, x, c: (g, x + 1, 1) if c == 0 else (g + 1, x, 0))
        for block in (first, other_second)
    ]
    starts = pulled(
        [
            ([first], [second, other_first], [], True),
            ([second], [first, other_second], [], True),
        ],
        [f32, f32],
        scale,
        shift,
    )
    got_a, both = lax.optimization_barrier((got_a, packed(scale, shift)))
    swap_a = swapped(got_a)
    got_b, *starts = lax.optimization_barrier((got_b, *starts))
    job_a = [([swap_a], [second, other_first, got_a, got_b], [], False)]
    [back_a] = pulled(job_a, [bf16], scale, shift, 1)
    [back_a] = pulled(job_a, [bf16], scale, shift, 0, back_a)
    got_b_again, back_a = lax.optimization_barrier((got_b, back_a))
    swap_b = swapped(got_b_again)
    [back_b] = pulled(
        [([swap_b], [second, other_first, got_a, got_b], [], False)], [bf16], scale, shift
    )
    home_a = sent(back_a, lambda g, x, c: (g, x + 1, 0) if c == 0 else (g - 1, x, 1))
    home_b = sent(back_b, lambda g, x, c: (g, x + 1, 1) if c == 0 else (g - 1, x, 0))
    first_total, second_total = pulled(
        [
            ([first], [got_a, got_b], starts[:1], False),
            ([second], [swap_a, swap_b], starts[1:], False),
        ],
        [f32, f32],
        both,
        None,
    )
    outputs = placed(first_total, home_a, None, 1)
    return tuple(placed(second_total, home_b, outputs, 0))


def by_arrays(images, texts, scale, shift):
    chips = lax.axis_size("in") // CORES
    f32, bf16 = jnp.float32, jnp.bfloat16
    back_texts = moved(texts, "grp", lambda i: i + 1)
    near_images = [moved(images, "in", lambda i, k=k: i - CORES * k) for k in range(1, chips)]
    images, texts = held([images, texts], scale, shift)
    core_images, core_texts = swapped(images), swapped(texts)
    far_images = [swapped(block) for block in near_images]
    far_texts = swapped(back_texts)
    own_texts = [texts, core_texts]
    group_images = [images, core_images] + near_images + far_images

    starts = pulled(
        [(near_images, own_texts, [], False)], [f32] * (chips - 1), scale, shift
    )
    [sent_texts] = pulled([([back_texts], group_images, [], False)], [bf16], scale, shift)
    sent_images = pulled(
        [(near_images, [back_texts, far_texts], starts, False)],
        [bf16] * (chips - 1),
        scale,
        shift,
    )
    sent_texts, *sent_images = lax.optimization_barrier((sent_texts, *sent_images))
    sent_images = [
        moved(block, "in", lambda i, k=k: i + CORES * k) for k, block in enumerate(sent_images, 1)
    ]
    sent_texts = moved(sent_texts, "grp", lambda i: i - 1)
    image_total, text_total = pulled(
        [
            ([images], own_texts + [back_texts, far_texts], [], True),
            ([texts], group_images, [], True),
        ],
        [f32, f32],
        scale,
        shift,
    )
    return tuple(summed([[image_total] + sent_images, [text_total, sent_texts]]))


def shards(images, texts, scale, shift):
    if lax.axis_size("in") == 2 * CORES:
        return by_roles(images, texts, scale, shift)
    return by_arrays(images, texts, scale, shift)


def solution(mesh):
    rows = P(("grp", "in"), None)
    return jax.shard_map(
        shards,
        mesh=mesh,
        in_specs=(rows, rows, P(), P()),
        out_specs=(rows, rows),
        check_vma=False,
    )
```
